768 devices in a mesh: owner: 32 (over x, y), hst: 24 (over z, core).
Axes of the slice: x: 4, y: 8, z: 12, core: 2. Of those that a mesh axis runs over, the one named last changes fastest.
Arguments:
- dense_input: bfloat16 [196608, 128], P(('owner', 'hst')), may hold values from -6 to 6
- owner_route: int32 [196608, 26, 1], P(('owner', 'hst')), may hold values from 0 to 31; in each aligned block of 6656 rows (0 to 6655, 6656 to 13311, ..., all dimensions but the last counted through in order) at most 416 rows name the same one
- local_row: int32 [196608, 26], P(('owner', 'hst')), may hold values from 0 to 3071
- labels: int32 [196608], P(('owner', 'hst')), may hold values 0 or 1
- table_rows: float32 [98304, 128], P('owner'), may hold values from -6 to 6
- adagrad_state: float32 [98304], P('owner'), may hold values from 1e-05 to 0.001
- cross_down: bfloat16 [3456, 512], replicated, may hold values from -0.109375 to 0.109375
- cross_up: bfloat16 [512, 3456], replicated, may hold values from -0.25 to 0.25
- cross_bias: float32 [3456], replicated, may hold values from -3 to 3
- out_weight: float32 [3456], replicated, may hold values from -0.109375 to 0.109375
Outputs:
- new_rows: float32 [98304, 128], P('owner')
- logits: float32 [196608], P(('owner', 'hst'))
The draws below stay inside these ranges and needn't reach their ends.
Inputs may be any that keep to these rules, and one draw needn't show every extreme that they name: `owner_route`: among the lookups of one device no owner index appears more than 416 times, and in every draw some device names some owner exactly 416 times.
All inputs are finite; a program needn't handle non-finite values. No bound on the sum of `labels` on one device may be relied on, other than what follows from the above.
Results may differ from the reference program's by a relative error of at most 0.0018.
The reference program's roundings to bfloat16 on the way (of `fetched`, `joined`, `lowrank`, `scaled`, `back_rank` and `emb_grad`) count: a program that leaves them out, or rounds other values in their place, can miss the bound.
Values may be sent and summed in bfloat16 or wider, within the bound.
A program may use at most 64 MiB of HBM per device.

```python
import math
import jax
import jax.numpy as jnp
import numpy as np
from jax import lax

EMB = 128
TABLES = 26
RANK = 512
SB = 256
ROWS_DEV = 3072
FEAT = 3456
SAMPLES = 196608
CAP = 416
N_OWNER = 32


def touch_ends(drawn, key, low, largest):
    dims = drawn.shape
    index_at = [jax.random.randint(jax.random.fold_in(key, axis), (), 0, dims[axis]) for axis in range(len(dims))]
    drawn = drawn.at[tuple(index_at)].set(low)
    longest = dims.index(max(dims))
    index_at[longest] = (index_at[longest] + 1) % dims[longest]
    return drawn.at[tuple(index_at)].set(largest)


def shard_levels(stream_key, shape, split, low, high):
    factor_of = 1.0
    for position, shards_of in split:
        steps = jax.random.uniform(jax.random.fold_in(jax.random.fold_in(stream_key, 6), position), (shards_of,), jnp.float32, low / len(split), high / len(split))
        factor_of = factor_of * jnp.repeat(jnp.exp(steps), shape[position] // shards_of).reshape((-1,) + (1,) * (len(shape) - 1 - position))
    return factor_of


def rank_table(number_of, slope):
    portions = [(1 << 20) // math.isqrt(grade ** slope) + 1 for grade in range(1, number_of + 1)]
    deviation = 1 + sum(portions) // (1 << 30)
    return np.cumsum(np.array([max(1, weight // deviation) for weight in portions]))


def skewed_ids(key, extent, amount, slope):
    table = rank_table(amount, slope)
    pick = jax.random.randint(jax.random.fold_in(key, 1), extent, 0, int(table[amount - 1]))
    standing = jnp.searchsorted(jnp.asarray(table, jnp.int32), pick, side="right")
    return jax.random.permutation(jax.random.fold_in(key, 2), amount)[standing].astype(jnp.int32)


def assign_block(key, own, number, rows, amount, top, reach, slope):
    ranking = jax.random.permutation(key, amount)
    crowded, usual = shares(amount, rows * top, reach, slope, True), shares(amount, rows * top, reach, slope, False)
    places = jnp.arange(amount)

    def named(sizes, rotation):
        used = int((sizes > 0).sum())
        fixed = max(1, used // 4)
        passed = fixed + (places - fixed + rotation * (used - fixed)) % max(1, amount - fixed)
        return jnp.zeros((amount,), jnp.int32).at[ranking[jnp.where(places < fixed, places, passed)]].set(jnp.asarray(sizes, jnp.int32))

    sizes = jnp.where(number % 4 == 0, named(crowded, number // 4), named(usual, number - number // 4 - 1))
    mixed = jax.random.permutation(jax.random.fold_in(own, 3), amount)
    giver, receiver = mixed[0:amount // 2 * 2:2], mixed[1:amount // 2 * 2:2]
    room = jnp.minimum(sizes[giver] - 1, reach - sizes[receiver]) // 2
    room = jnp.where((giver == ranking[0]) | (receiver == ranking[0]) | (sizes[receiver] == 0), 0, jnp.maximum(room, 0))
    passed = jax.random.randint(jax.random.fold_in(own, 4), (amount // 2,), 0, 1 << 20) % (room + 1)
    sizes = sizes.at[giver].add(-passed).at[receiver].add(passed)
    items = jnp.searchsorted(jnp.cumsum(sizes), jnp.arange(rows * top), side="right").astype(jnp.int32)
    table = items.reshape(top, rows).T
    table = table[jax.random.permutation(jax.random.fold_in(own, 1), rows)]
    rotation = jax.random.randint(jax.random.fold_in(own, 2), (rows, 1), 0, top)
    return jnp.take_along_axis(table, (jnp.arange(top)[None, :] + rotation) % top, axis=1)


def shares(amount, total, reach, lean, full):
    weights = [(1 << 20) // math.isqrt(grade ** lean) + 1 for grade in range(1, amount + 1)]
    largest = reach if full else min(reach, max(-(-total // amount), total * weights[0] // sum(weights)))
    least = 1 if total - largest >= amount - 1 else 0
    holding, spare = [largest] + [least] * (amount - 1), total - largest - least * (amount - 1)
    while spare > 0:
        free = [i for i in range(1, amount) if holding[i] < largest] or [i for i in range(1, amount) if holding[i] < reach]
        mass, left = sum([weights[i] for i in free]), spare
        for i in free:
            more = min(reach - holding[i], max(1, left * weights[i] // mass), spare)
            holding[i] = holding[i] + more
            spare = spare - more
    return np.array(holding)


def scatter_about(stream_key, dims, width, reach, cuts=(), held_as=jnp.bfloat16):
    array = width * jax.random.normal(stream_key, dims, jnp.float32)
    if cuts:
        array = array * shard_levels(stream_key, dims, cuts, -0.22, 0.18)
    return jnp.clip(array, -reach, reach).astype(held_as)


def setup_inputs(seed: int = 0) -> dict:
    splits = jax.random.split(jax.random.key(seed), 11)
    dense_input = scatter_about(splits[0], (SAMPLES, EMB), 1.0, 6.0, ((0, 768),))
    owner_route_keys = jax.random.split(jax.random.fold_in(splits[1], 1), SAMPLES * TABLES // (SB * TABLES))
    owner_route_turns = jax.random.permutation(jax.random.fold_in(splits[1], 3), SAMPLES * TABLES // (SB * TABLES))
    owner_route = jax.vmap(lambda own, number: assign_block(jax.random.fold_in(splits[1], 2), own, number, SB * TABLES, N_OWNER, 1, CAP, 2))(owner_route_keys, owner_route_turns).reshape((SAMPLES, TABLES, 1))
    local_row = touch_ends(skewed_ids(splits[2], (SAMPLES, TABLES), ROWS_DEV, 2), jax.random.fold_in(splits[2], 3), 0, ROWS_DEV - 1).astype(jnp.int32)
    labels = touch_ends((jax.random.randint(splits[3], (SAMPLES,), 0, 4) < 1).astype(jnp.int32), jax.random.fold_in(splits[3], 1), 0, 1)
    table_rows = scatter_about(splits[4], (N_OWNER * ROWS_DEV, EMB), 1.0, 6.0, ((0, 32),), jnp.float32)
    adagrad_state = jnp.clip(jnp.exp(math.log(0.001) - 4.6051703 * jax.random.uniform(splits[5], (N_OWNER * ROWS_DEV,), jnp.float32) ** shard_levels(splits[5], (N_OWNER * ROWS_DEV,), ((0, 32),), -0.2, 0.2)), 9.999999747378752e-06, 0.001)
    cross_down = scatter_about(splits[6], (FEAT, RANK), FEAT ** -0.5, 0.109375)
    cross_up = scatter_about(splits[7], (RANK, FEAT), RANK ** -0.5, 0.25)
    cross_bias = scatter_about(splits[8], (FEAT,), 0.5, 3.0, (), jnp.float32)
    out_weight = scatter_about(splits[9], (FEAT,), FEAT ** -0.5, 0.109375, (), jnp.float32)
    return dict(dense_input=dense_input, owner_route=owner_route, local_row=local_row, labels=labels, table_rows=table_rows, adagrad_state=adagrad_state, cross_down=cross_down, cross_up=cross_up, cross_bias=cross_bias, out_weight=out_weight)


learn_rate = 0.1

def reference(dense_input, owner_route, local_row, labels, table_rows, adagrad_state, cross_down, cross_up, cross_bias, out_weight):
    rows_bf = table_rows.astype(jnp.bfloat16)
    block_rows = SAMPLES // N_OWNER
    row_id = (owner_route.reshape(SAMPLES, TABLES) * ROWS_DEV + local_row).astype(jnp.int32)
    emb_down = cross_down[EMB:, :]

    def visit(carry, pieces):
        dense_part, id_part, label_part = pieces
        flat_ids = id_part.reshape(block_rows * TABLES)
        fetched = rows_bf[flat_ids].reshape(block_rows, TABLES * EMB)
        joined = jnp.concatenate([dense_part, fetched], axis=1)
        lowrank = jnp.dot(joined, cross_down, preferred_element_type=jnp.float32).astype(jnp.bfloat16)
        mixing = jnp.dot(lowrank, cross_up, preferred_element_type=jnp.float32) + cross_bias[None, :]
        joined_f = joined.astype(jnp.float32)
        crossed = joined_f * (1.0 + mixing)
        logit_part = lax.optimization_barrier(jnp.sum(crossed * out_weight[None, :], axis=1))
        logit_grad = jax.nn.sigmoid(logit_part) - label_part.astype(jnp.float32)
        upstream = logit_grad[:, None] * out_weight[None, :]
        scaled = (upstream * joined_f).astype(jnp.bfloat16)
        back_rank = jnp.dot(scaled, cross_up.T, preferred_element_type=jnp.float32).astype(jnp.bfloat16)
        emb_grad = upstream[:, EMB:] * (1.0 + mixing[:, EMB:]) + jnp.dot(back_rank, emb_down.T, preferred_element_type=jnp.float32)
        emb_grad = emb_grad.astype(jnp.bfloat16).reshape(block_rows * TABLES, EMB)
        carry = carry.at[flat_ids].add(emb_grad.astype(jnp.float32))
        return (carry, logit_part)
    start_grad = jnp.zeros((N_OWNER * ROWS_DEV, EMB), jnp.float32)
    row_grad, logit_blocks = lax.scan(visit, start_grad, (dense_input.reshape(N_OWNER, block_rows, EMB), row_id.reshape(N_OWNER, block_rows, TABLES), labels.reshape(N_OWNER, block_rows)))
    fresh_state = adagrad_state + lax.optimization_barrier(jnp.mean(row_grad * row_grad, axis=1))
    new_rows = table_rows - learn_rate * row_grad / jnp.sqrt(fresh_state)[:, None]
    return (new_rows, logit_blocks.reshape(SAMPLES))
```

```python
import functools
import jax
import jax.numpy as jnp
from jax import lax
from jax.experimental import pallas as pl
from jax.experimental.pallas import tpu as pltpu
from jax.sharding import PartitionSpec as P

XS, YS, ZS, OWNERS = 4, 8, 12, 32
ROWS = 3072
HALF, PAIR, SUB = 1536, 512, 256
RIGHT, LEFT = 16, 15


def place():
    o = lax.axis_index("owner")
    h = lax.axis_index("hst")
    x, y, z, core = o // YS, o % YS, h // 2, h % 2
    diag = (x + y) % 4
    at_a = 4 * y + diag
    at_b = 4 * ((3 * (y - diag + 8)) % 8) + diag
    return o, h, z, core, (at_a, at_b)


def owner_at(cycle, position):
    p = (position + 2 * OWNERS) % OWNERS
    q, r = p // 4, p % 4
    if cycle == 0:
        return ((r - q + 8) % 4) * YS + q
    return (q % 4) * YS + (3 * q + r) % 8


def greet(devices):
    barrier = pltpu.get_barrier_semaphore()
    for d in devices:
        pl.semaphore_signal(barrier, inc=1, device_id=d, device_id_type=pl.DeviceIdType.MESH)
    pl.semaphore_wait(barrier, len(devices))


def send(src, dst, ssem, rsem, device):
    return pltpu.make_async_remote_copy(
        src_ref=src, dst_ref=dst, send_sem=ssem, recv_sem=rsem,
        device_id=device, device_id_type=pl.DeviceIdType.MESH)


STREAMS = [(c, d) for c in (0, 1) for d in (0, 1)]


def gather_kernel(tab, out, own_sem, ring_s, ring_r, sib_s, sib_r, z_s, z_r, zs_s, zs_r):
    o, h, z, core, at = place()
    color = z % 3
    sib = (o, h + 1 - 2 * core)
    up = (o, ((z + 1) % ZS) * 2 + core)
    down = (o, ((z + ZS - 1) % ZS) * 2 + core)
    nxt = [[(owner_at(c, at[c] + 1), h), (owner_at(c, at[c] - 1), h)] for c in (0, 1)]
    greet([sib, up, down, nxt[0][0], nxt[0][1], nxt[1][0], nxt[1][1]])
    base = core * HALF
    pair_row = [base + ((color + 1) % 3) * PAIR, base + ((color + 2) % 3) * PAIR]
    miss_row = [base + color * PAIR, base + color * PAIR + SUB]
    zdev = [up, down]

    own = pltpu.make_async_copy(tab, out.at[pl.ds(o * ROWS, ROWS)], own_sem)
    own.start()

    def source(c, d, s):
        return owner_at(c, at[c] - 1 - s) if d == 0 else owner_at(c, at[c] + 1 + s)

    def rows(owner, row, n):
        return out.at[pl.ds(pl.multiple_of(owner * ROWS + row, SUB), n)]

    def ring(c, d, s, src_ref):
        w = c * 2 + d
        src = source(c, d, s - 1)
        dst = rows(src, pair_row[c], PAIR)
        return send(dst if src_ref is None else src_ref, dst, ring_s.at[w, s], ring_r.at[w, s], nxt[c][d])

    def sibling(c, d, s):
        w = c * 2 + d
        ref = rows(source(c, d, s), pair_row[c], PAIR)
        return send(ref, ref, sib_s.at[w, s], sib_r.at[w, s], sib)

    def zed(c, d, s):
        w = c * 2 + d
        ref = rows(source(c, d, s), pair_row[c] + c * SUB, SUB)
        return send(ref, ref, z_s.at[w, s], z_r.at[w, s], zdev[c])

    def zsib(c, d, s):
        w = c * 2 + d
        ref = rows(source(c, d, s), miss_row[c], SUB)
        return send(ref, ref, zs_s.at[w, s], zs_r.at[w, s], sib)

    for c, d in STREAMS:
        first = tab.at[pl.ds(pl.multiple_of(pair_row[c], SUB), PAIR)]
        ring(c, d, 0, first).start()

    def arrive(c, d, s, last):
        w = c * 2 + d
        ref = rows(source(c, d, s), pair_row[c], PAIR)
        pltpu.make_async_copy(ref, ref, ring_r.at[w, s]).wait()
        if not last:
            ring(c, d, s + 1, None).start()
        zed(c, d, s).start()
        sibling(c, d, s).start()

    def zarrive(c, d, s):
        w = c * 2 + d
        ref = rows(source(c, d, s), miss_row[c], SUB)
        pltpu.make_async_copy(ref, ref, z_r.at[w, s]).wait()
        zsib(c, d, s).start()

    def step(s, _):
        for c, d in STREAMS:
            arrive(c, d, s, False)

        @pl.when(s > 0)
        def _():
            for c, d in STREAMS:
                zarrive(c, d, s - 1)
        return 0

    lax.fori_loop(0, LEFT - 1, step, 0)
    s = LEFT - 1
    for c, d in STREAMS:
        arrive(c, d, s, d == 1)
    for c, d in STREAMS:
        zarrive(c, d, s - 1)
    for c in (0, 1):
        arrive(c, 0, RIGHT - 1, True)
    for c, d in STREAMS:
        zarrive(c, d, s)
    for c in (0, 1):
        zarrive(c, 0, RIGHT - 1)

    def finish(c, d, s):
        w = c * 2 + d
        ring(c, d, s, None).wait_send()
        sibling(c, d, s).wait_send()
        zed(c, d, s).wait_send()
        zsib(c, d, s).wait_send()
        a = rows(source(c, d, s), (1 - core) * HALF, PAIR)
        pltpu.make_async_copy(a, a, sib_r.at[w, s]).wait()
        a = rows(source(c, d, s), (1 - core) * HALF, SUB)
        pltpu.make_async_copy(a, a, zs_r.at[w, s]).wait()

    def end(s, _):
        for c, d in STREAMS:
            finish(c, d, s)
        return 0

    lax.fori_loop(0, LEFT, end, 0)
    for c in (0, 1):
        finish(c, 0, RIGHT - 1)
    own.wait()


def gather_tables(tab):
    return pl.pallas_call(
        gather_kernel,
        out_shape=jax.ShapeDtypeStruct((OWNERS * ROWS, 128), jnp.bfloat16),
        in_specs=[pl.BlockSpec(memory_space=pl.ANY)],
        out_specs=pl.BlockSpec(memory_space=pl.ANY),
        scratch_shapes=[pltpu.SemaphoreType.DMA(())] + [pltpu.SemaphoreType.DMA((4, 16))] * 8,
        compiler_params=pltpu.CompilerParams(collective_id=0, has_side_effects=True),
        name="gather_tables",
    )(tab)


LOOKUPS = 6656
TABLE = OWNERS * ROWS


def scatter_kernel(ids, g, out, acc, gf, stage, sem):
    def clear(i, _):
        acc[pl.ds(pl.multiple_of(i * 512, 512), 512), :] = jnp.zeros((512, 128), jnp.float32)
        return 0
    lax.fori_loop(0, TABLE // 512, clear, 0)

    def widen(i, _):
        r = pl.ds(pl.multiple_of(i * 128, 128), 128)
        gf[r, :] = g[r, :].astype(jnp.float32)
        return 0
    lax.fori_loop(0, LOOKUPS // 128, widen, 0)

    def add(i, _):
        for k in range(8):
            j = i * 8 + k
            row = ids[j]
            acc[pl.ds(row, 1), :] = acc[pl.ds(row, 1), :] + gf[pl.ds(j, 1), :]
        return 0
    lax.fori_loop(0, LOOKUPS // 8, add, 0)

    def copy(i):
        slot = i % 2
        return pltpu.make_async_copy(stage.at[slot], out.at[pl.ds(pl.multiple_of(i * ROWS, ROWS), ROWS)], sem.at[slot])

    def write(i, _):
        @pl.when(i >= 2)
        def _():
            copy(i - 2).wait()

        def narrow(k, _):
            r = pl.multiple_of(k * 256, 256)
            stage[i % 2, pl.ds(r, 256), :] = acc[pl.ds(pl.multiple_of(i * ROWS + r, 256), 256), :].astype(jnp.bfloat16)
            return 0
        lax.fori_loop(0, ROWS // 256, narrow, 0)
        copy(i).start()
        return 0
    lax.fori_loop(0, OWNERS, write, 0)
    copy(OWNERS - 2).wait()
    copy(OWNERS - 1).wait()


def scatter_rows(ids, g):
    return pl.pallas_call(
        scatter_kernel,
        out_shape=jax.ShapeDtypeStruct((TABLE, 128), jnp.bfloat16),
        in_specs=[pl.BlockSpec(memory_space=pltpu.SMEM), pl.BlockSpec(memory_space=pltpu.VMEM)],
        out_specs=pl.BlockSpec(memory_space=pl.ANY),
        scratch_shapes=[
            pltpu.VMEM((TABLE, 128), jnp.float32), pltpu.VMEM((LOOKUPS, 128), jnp.float32),
            pltpu.VMEM((2, ROWS, 128), jnp.bfloat16), pltpu.SemaphoreType.DMA((2,))],
        compiler_params=pltpu.CompilerParams(vmem_limit_bytes=60 * 1024 * 1024),
        name="scatter_rows",
    )(ids, g)


CHUNK = 128
AHEAD = 4


def reduce_kernel(part, out, own_m, own_z, sib_m, sib_z, ring_b, z_b, fin, zr, tot,
                  lm, lz, sm_s, sm_r, sz_s, sz_r, rg_s, rg_r, zz_s, zz_r, c_s, c_r, b_s, b_r, f_s, f_r, t_s):
    o, h, z, core, at = place()
    color = z % 3
    sib = (o, h + 1 - 2 * core)
    zs = [(o, ((z + k) % ZS) * 2 + core) for k in range(ZS)]
    nxt = [[(owner_at(c, at[c] + 1), h), (owner_at(c, at[c] - 1), h)] for c in (0, 1)]
    greet([sib] + zs[1:] + [nxt[0][0], nxt[0][1], nxt[1][0], nxt[1][1]])
    zdev = [zs[ZS - 1], zs[1]]
    pair = [((color + 1) % 3) * PAIR, ((color + 2) % 3) * PAIR]
    miss = [color * PAIR, color * PAIR + SUB]

    def dest(c, d, s):
        return owner_at(c, at[c] + RIGHT - s) if d == 0 else owner_at(c, at[c] - LEFT + s)

    def src(c, d, s, side, row, n):
        return part.at[pl.ds(pl.multiple_of(dest(c, d, s) * ROWS + side * HALF + row, SUB), n)]

    def loads(c, d, s):
        w = c * 2 + d
        other = 1 - core
        return (
            pltpu.make_async_copy(src(c, d, s, core, miss[c], SUB), own_z.at[w, s], lz.at[w, s]),
            send(src(c, d, s, other, miss[c], SUB), sib_z.at[w, s], sz_s.at[w, s], sz_r.at[w, s], sib),
            pltpu.make_async_copy(src(c, d, s, core, pair[c], PAIR), own_m.at[w, s], lm.at[w, s]),
            send(src(c, d, s, other, pair[c], PAIR), sib_m.at[w, s], sm_s.at[w, s], sm_r.at[w, s], sib),
        )

    def fetch(c, d, s):
        for copy in loads(c, d, s):
            copy.start()

    def zcopy(c, d, s):
        w = c * 2 + d
        return send(own_z.at[w, s], z_b.at[w, s], zz_s.at[w, s], zz_r.at[w, s], zdev[c])

    def rcopy(c, d, s):
        w = c * 2 + d
        return send(own_m.at[w, s], ring_b.at[w, s], rg_s.at[w, s], rg_r.at[w, s], nxt[c][d])

    def zpart(c, d, s):
        w = c * 2 + d
        l = loads(c, d, s)
        l[0].wait()
        l[1].wait_recv()

        def add(i, _):
            r = pl.ds(pl.multiple_of(i * 64, 64), 64)
            own_z[w, s, r, :] = (own_z[w, s, r, :].astype(jnp.float32) + sib_z[w, s, r, :].astype(jnp.float32)).astype(jnp.bfloat16)
            return 0
        lax.fori_loop(0, SUB // 64, add, 0)
        zcopy(c, d, s).start()

    def total(c, d, s, more, final=False):
        w = c * 2 + d
        l = loads(c, d, s)
        l[2].wait()
        l[3].wait_recv()
        zcopy(c, d, s).wait_recv()
        for w2, s2, copy in more:
            copy.wait_recv()

        def add(i, _, with_z, first):
            r = pl.ds(pl.multiple_of(first + i * 64, 64), 64)
            t = own_m[w, s, r, :].astype(jnp.float32) + sib_m[w, s, r, :].astype(jnp.float32)
            if with_z:
                t = t + z_b[w, s, pl.ds(pl.multiple_of(i * 64, 64), 64), :].astype(jnp.float32)
            for w2, s2, _copy in more:
                t = t + ring_b[w2, s2, r, :].astype(jnp.float32)
            t = t.astype(jnp.bfloat16)
            if final:
                fin[c, r, :] = t
            else:
                own_m[w, s, r, :] = t
            return 0
        lax.fori_loop(0, SUB // 64, lambda i, x: add(i, x, c == 0, 0), 0)
        lax.fori_loop(0, SUB // 64, lambda i, x: add(i, x, c == 1, SUB), 0)

    FINAL = RIGHT

    def on(c, d, s):
        total(c, d, s, [(c * 2 + d, s - 1, rcopy(c, d, s - 1))])
        rcopy(c, d, s).start()

    for s in range(AHEAD):
        for c, d in STREAMS:
            fetch(c, d, s)
    for s in range(2):
        for c, d in STREAMS:
            zpart(c, d, s)
    for c, d in STREAMS:
        total(c, d, 0, [])
        rcopy(c, d, 0).start()

    def step(s, _):
        @pl.when(s + AHEAD - 1 < LEFT)
        def _():
            for c, d in STREAMS:
                fetch(c, d, s + AHEAD - 1)

        @pl.when(jnp.logical_and(s + AHEAD - 1 >= LEFT, s + AHEAD - 1 <= RIGHT))
        def _():
            for c in (0, 1):
                fetch(c, 0, s + AHEAD - 1)

        @pl.when(s + 1 < LEFT)
        def _():
            for c, d in STREAMS:
                zpart(c, d, s + 1)

        @pl.when(s + 1 >= LEFT)
        def _():
            for c in (0, 1):
                zpart(c, 0, s + 1)
        for c, d in STREAMS:
            on(c, d, s)
        return 0

    lax.fori_loop(1, LEFT, step, 0)
    for c in (0, 1):
        zpart(c, 0, RIGHT)
    for c in (0, 1):
        on(c, 0, RIGHT - 1)
    for c in (1, 0):
        total(c, 0, FINAL, [(c * 2, RIGHT - 1, rcopy(c, 0, RIGHT - 1)), (c * 2 + 1, LEFT - 1, rcopy(c, 1, LEFT - 1))], True)

    hops = [3, 6, 9, 1, 4, 7, 10]

    def scatter(k):
        hop = hops[k]
        to = (z + hop) % ZS
        ref = fin.at[0 if k < 3 else 1, pl.ds(pl.multiple_of((to // 3) * CHUNK, CHUNK), CHUNK)]
        return send(ref, zr.at[k], c_s.at[k], c_r.at[k], zs[hop])
    order = [3, 6, 0, 2, 4, 5, 1]
    for k in order:
        scatter(k).start()
    mine = pl.ds(pl.multiple_of((z // 3) * CHUNK, CHUNK), CHUNK)
    for k in range(7):
        scatter(k).wait_recv()
    t = fin[0, mine, :].astype(jnp.float32)
    for k in range(7):
        t = t + zr[k].astype(jnp.float32)
    tot[...] = t.astype(jnp.bfloat16)

    def chunk_rows(layer):
        return out.at[pl.ds(pl.multiple_of(core * HALF + ((layer % 3 + 1) % 3) * PAIR + (layer // 3) * CHUNK, CHUNK), CHUNK)]

    def spread(k):
        return send(tot, chunk_rows(z), b_s.at[k], b_r.at[k], zs[k])

    def arrived(k):
        ref = chunk_rows((z + ZS - k) % ZS)
        return send(ref, ref, f_s.at[k], f_r.at[k], sib)
    far = [1, 11, 2, 10, 3, 9, 4, 8, 5, 7, 6]
    for k in far:
        spread(k).start()
    first = send(tot, chunk_rows(z), f_s.at[0], f_r.at[0], sib)
    first.start()
    keep = pltpu.make_async_copy(tot, chunk_rows(z), t_s)
    keep.start()
    for k in far:
        ref = chunk_rows((z + ZS - k) % ZS)
        pltpu.make_async_copy(ref, ref, b_r.at[k]).wait()
        arrived(k).start()
    keep.wait()
    first.wait()
    for k in far:
        spread(k).wait_send()
        arrived(k).wait()
    for k in range(7):
        scatter(k).wait_send()

    def end(c, d, s, ring):
        l = loads(c, d, s)
        l[1].wait_send()
        l[3].wait_send()
        zcopy(c, d, s).wait_send()
        if ring:
            rcopy(c, d, s).wait_send()

    def ends(s, _):
        for c, d in STREAMS:
            end(c, d, s, True)
        return 0
    lax.fori_loop(0, LEFT, ends, 0)
    for c in (0, 1):
        end(c, 0, RIGHT - 1, True)
        end(c, 0, RIGHT, False)


def reduce_tables(part):
    bf = jnp.bfloat16
    dma = lambda *n: pltpu.SemaphoreType.DMA(n)
    n = RIGHT + 1
    return pl.pallas_call(
        reduce_kernel,
        out_shape=jax.ShapeDtypeStruct((ROWS, 128), bf),
        in_specs=[pl.BlockSpec(memory_space=pl.ANY)],
        out_specs=pl.BlockSpec(memory_space=pl.ANY),
        scratch_shapes=[
            pltpu.VMEM((4, n, PAIR, 128), bf), pltpu.VMEM((4, n, SUB, 128), bf),
            pltpu.VMEM((4, n, PAIR, 128), bf), pltpu.VMEM((4, n, SUB, 128), bf),
            pltpu.VMEM((4, RIGHT, PAIR, 128), bf), pltpu.VMEM((4, n, SUB, 128), bf),
            pltpu.VMEM((2, PAIR, 128), bf), pltpu.VMEM((7, CHUNK, 128), bf), pltpu.VMEM((CHUNK, 128), bf),
        ] + [dma(4, n)] * 10 + [dma(7)] * 2 + [dma(ZS)] * 4 + [dma()],
        compiler_params=pltpu.CompilerParams(collective_id=1, has_side_effects=True, vmem_limit_bytes=56 * 1024 * 1024),
        name="reduce_tables",
    )(part)


learn_rate = 0.1


def body(
    dense_input,
    owner_route,
    local_row,
    labels,
    table_rows,
    adagrad_state,
    cross_down,
    cross_up,
    cross_bias,
    out_weight,
):
    samples, emb_width = dense_input.shape
    tables = local_row.shape[1]
    lookups = samples * tables
    ids = (owner_route.reshape(samples, tables) * ROWS + local_row).reshape(lookups)
    full = gather_tables(table_rows.astype(jnp.bfloat16))
    fetched = full[ids].reshape(samples, tables * emb_width)
    joined = jnp.concatenate([dense_input, fetched], axis=1)
    lowrank = jnp.dot(joined, cross_down, preferred_element_type=jnp.float32).astype(jnp.bfloat16)
    mixing = jnp.dot(lowrank, cross_up, preferred_element_type=jnp.float32) + cross_bias[None, :]
    joined_f = joined.astype(jnp.float32)
    crossed = joined_f * (1.0 + mixing)
    logits = jnp.sum(crossed * out_weight[None, :], axis=1)
    logit_grad = jax.nn.sigmoid(logits) - labels.astype(jnp.float32)
    upstream = logit_grad[:, None] * out_weight[None, :]
    scaled = (upstream * joined_f).astype(jnp.bfloat16)
    back_rank = lax.dot_general(
        scaled, cross_up, (((1,), (1,)), ((), ())), preferred_element_type=jnp.float32
    ).astype(jnp.bfloat16)
    emb_down = cross_down[emb_width:, :]
    emb_grad = upstream[:, emb_width:] * (1.0 + mixing[:, emb_width:]) + lax.dot_general(
        back_rank, emb_down, (((1,), (1,)), ((), ())), preferred_element_type=jnp.float32
    )
    emb_grad = emb_grad.astype(jnp.bfloat16).reshape(lookups, emb_width)
    row_grad = reduce_tables(scatter_rows(ids, emb_grad)).astype(jnp.float32)
    fresh_state = adagrad_state + jnp.mean(row_grad * row_grad, axis=1)
    new_rows = table_rows - learn_rate * row_grad / jnp.sqrt(fresh_state)[:, None]
    return (new_rows, logits)


def solution(mesh):
    in_specs = (
        P(("owner", "hst"), None),
        P(("owner", "hst"), None, None),
        P(("owner", "hst"), None),
        P(("owner", "hst")),
        P("owner", None),
        P("owner"),
        P(),
        P(),
        P(),
        P(),
    )
    out_specs = (P("owner", None), P(("owner", "hst")))
    return jax.shard_map(body, mesh=mesh, in_specs=in_specs, out_specs=out_specs, check_vma=False)
```

```python
import heapq
import jax
import jax.numpy as jnp
from jax import lax
from jax.experimental import pallas as pl
from jax.experimental.pallas import tpu as pltpu
from jax.sharding import PartitionSpec as P

XS, YS, ZS, OWNERS = 4, 8, 12, 32
ROWS = 3072
HALF, PAIR, SUB = 1536, 512, 256
TABLE = OWNERS * ROWS
STEPS = ((1, 0), (-1, 0), (0, 1), (0, -1))


def trees():
    children = [[[] for _ in range(OWNERS)] for _ in range(2)]

    def grow(plan, parent, direction):
        i, j = parent[0] + STEPS[direction][0], parent[1] + STEPS[direction][1]
        children[plan][parent[0] % XS * YS + parent[1] % YS].append((i % XS * YS + j % YS, direction))
        return i, j

    def line(plan, start, direction, count):
        for _ in range(count):
            start = grow(plan, start, direction)
        return start

    def over_x(plan, start, up):
        line(plan, start, 0, up)
        line(plan, start, 1, 3 - up)

    over_x(0, (0, 0), 2)
    for i in range(XS):
        far = line(0, (i, 0), 2, 4 if i == 0 else 3)
        line(0, (i, 0), 3, 3)
        if i == 0:
            over_x(0, far, 1)
    line(1, (0, 0), 2, 3)
    line(1, (0, 0), 3, 4)
    for j in range(YS):
        over_x(1, (0, j), 2 - j % 2)
    return children


def depths(children, n):
    return 1 + max([depths(children, m) for m, _ in children[n]], default=0)


def arrivals(children):
    busy, queue, order = [0.0] * 4, [(0.0, 0, 0, 0), (0.0, 0, 1, 0)], []
    while queue:
        now, _, plan, n = heapq.heappop(queue)
        if n:
            order.append((plan, n))
        for m, direction in sorted(children[plan][n], key=lambda e: -depths(children[plan], e[0])):
            busy[direction] = max(now, busy[direction]) + 2.6
            heapq.heappush(queue, (busy[direction] + 2.5, len(order) * 64 + m, plan, m))
    return order


TREES = trees()
ORDER = arrivals(TREES)


def place():
    o = lax.axis_index("owner")
    h = lax.axis_index("hst")
    x, y, z, core = o // YS, o % YS, h // 2, h % 2
    near = [(((x + i + XS) % XS) * YS + (y + j + YS) % YS, h) for i, j in STEPS]
    owners = [((x + XS - n // YS) % XS) * YS + (y + YS - n % YS) % YS for n in range(OWNERS)]
    return o, h, z, core, near, owners


def greet(devices):
    barrier = pltpu.get_barrier_semaphore()
    for d in devices:
        pl.semaphore_signal(barrier, inc=1, device_id=d, device_id_type=pl.DeviceIdType.MESH)
    pl.semaphore_wait(barrier, len(devices))


def send(src, dst, ssem, rsem, device):
    return pltpu.make_async_remote_copy(
        src_ref=src, dst_ref=dst, send_sem=ssem, recv_sem=rsem,
        device_id=device, device_id_type=pl.DeviceIdType.MESH)


Z_LAG = 6


def gather_kernel(tab, out, own_sem, ring_s, ring_r, sib_s, sib_r, z_s, z_r, zs_s, zs_r):
    o, h, z, core, near, owners = place()
    color = z % 3
    sib = (o, h + 1 - 2 * core)
    zdev = [(o, ((z + 1) % ZS) * 2 + core), (o, ((z + ZS - 1) % ZS) * 2 + core)]
    greet([sib] + zdev + near)
    base = core * HALF
    pair_row = [base + ((color + 1) % 3) * PAIR, base + ((color + 2) % 3) * PAIR]
    miss_row = [base + color * PAIR, base + color * PAIR + SUB]

    own = pltpu.make_async_copy(tab, out.at[pl.ds(pl.multiple_of(o * ROWS, ROWS), ROWS)], own_sem)
    own.start()

    def rows(n, row, count):
        return out.at[pl.ds(pl.multiple_of(owners[n] * ROWS + row, SUB), count)]

    def ring(p, n, m, direction):
        ref = rows(n, pair_row[p], PAIR)
        src = ref if n else tab.at[pl.ds(pl.multiple_of(pair_row[p], SUB), PAIR)]
        return send(src, ref, ring_s.at[p], ring_r.at[p, m], near[direction])

    def sibling(p, n):
        ref = rows(n, pair_row[p], PAIR)
        return send(ref, ref, sib_s.at[p], sib_r.at[p], sib)

    def zed(p, n):
        ref = rows(n, pair_row[p] + p * SUB, SUB)
        return send(ref, ref, z_s.at[p], z_r.at[p, n], zdev[p])

    def zsib(p, n):
        ref = rows(n, miss_row[p], SUB)
        return send(ref, ref, zs_s.at[p], zs_r.at[p], sib)

    def onward(p, n):
        for m, direction in sorted(TREES[p][n], key=lambda e: -depths(TREES[p], e[0])):
            ring(p, n, m, direction).start()

    def await_(ref, sem):
        pltpu.make_async_copy(ref, ref, sem).wait()

    for p in (0, 1):
        onward(p, 0)
    for k in range(len(ORDER) + Z_LAG):
        if k < len(ORDER):
            p, n = ORDER[k]
            await_(rows(n, pair_row[p], PAIR), ring_r.at[p, n])
            onward(p, n)
            zed(p, n).start()
            sibling(p, n).start()
        if k >= Z_LAG:
            p, n = ORDER[k - Z_LAG]
            await_(rows(n, miss_row[p], SUB), z_r.at[p, n])
            zsib(p, n).start()
    whole, half = out.at[pl.ds(0, 31 * PAIR)], out.at[pl.ds(0, 31 * SUB)]
    for p in (0, 1):
        await_(whole, sib_r.at[p])
        await_(half, zs_r.at[p])
        for sem in (ring_s, sib_s):
            await_(whole, sem.at[p])
        for sem in (z_s, zs_s):
            await_(half, sem.at[p])
    own.wait()


def dma(*shape):
    return pltpu.SemaphoreType.DMA(shape)


def gather_tables(tab):
    return pl.pallas_call(
        gather_kernel,
        out_shape=jax.ShapeDtypeStruct((TABLE, 128), jnp.bfloat16),
        in_specs=[pl.BlockSpec(memory_space=pl.ANY)],
        out_specs=pl.BlockSpec(memory_space=pl.ANY),
        scratch_shapes=[dma()] + [dma(2), dma(2, OWNERS), dma(2), dma(2), dma(2), dma(2, OWNERS), dma(2), dma(2)],
        compiler_params=pltpu.CompilerParams(collective_id=2, has_side_effects=True),
        cost_estimate=pl.CostEstimate(flops=0, bytes_accessed=50000000, transcendentals=0),
        name="gather_tables",
    )(tab)


LOOKUPS = 6656


def scatter_kernel(ids, g, out, acc, gf, stage, sem):
    def clear(i, _):
        acc[pl.ds(pl.multiple_of(i * 512, 512), 512), :] = jnp.zeros((512, 128), jnp.float32)
        return 0
    lax.fori_loop(0, TABLE // 512, clear, 0)

    def widen(i, _):
        r = pl.ds(pl.multiple_of(i * 128, 128), 128)
        gf[r, :] = g[r, :].astype(jnp.float32)
        return 0
    lax.fori_loop(0, LOOKUPS // 128, widen, 0)

    def add(i, _):
        for k in range(8):
            j = i * 8 + k
            row = ids[j]
            acc[pl.ds(row, 1), :] = acc[pl.ds(row, 1), :] + gf[pl.ds(j, 1), :]
        return 0
    lax.fori_loop(0, LOOKUPS // 8, add, 0)

    def copy(i):
        slot = i % 2
        return pltpu.make_async_copy(stage.at[slot], out.at[pl.ds(pl.multiple_of(i * ROWS, ROWS), ROWS)], sem.at[slot])

    def write(i, _):
        @pl.when(i >= 2)
        def _():
            copy(i - 2).wait()

        def narrow(k, _):
            r = pl.multiple_of(k * 256, 256)
            stage[i % 2, pl.ds(r, 256), :] = acc[pl.ds(pl.multiple_of(i * ROWS + r, 256), 256), :].astype(jnp.bfloat16)
            return 0
        lax.fori_loop(0, ROWS // 256, narrow, 0)
        copy(i).start()
        return 0
    lax.fori_loop(0, OWNERS, write, 0)
    copy(OWNERS - 2).wait()
    copy(OWNERS - 1).wait()


def scatter_rows(ids, g):
    return pl.pallas_call(
        scatter_kernel,
        out_shape=jax.ShapeDtypeStruct((TABLE, 128), jnp.bfloat16),
        in_specs=[pl.BlockSpec(memory_space=pltpu.SMEM), pl.BlockSpec(memory_space=pltpu.VMEM)],
        out_specs=pl.BlockSpec(memory_space=pl.ANY),
        scratch_shapes=[
            pltpu.VMEM((TABLE, 128), jnp.float32), pltpu.VMEM((LOOKUPS, 128), jnp.float32),
            pltpu.VMEM((2, ROWS, 128), jnp.bfloat16), pltpu.SemaphoreType.DMA((2,))],
        compiler_params=pltpu.CompilerParams(vmem_limit_bytes=60 * 1024 * 1024),
        name="scatter_rows",
    )(ids, g)


CHUNK = 128
LOAD_AHEAD, Z_AHEAD = 20, 10
BACK = [e for e in reversed(ORDER)] + [(0, 0), (1, 0)]


def reduce_kernel(part, out, own_m, own_z, sib_m, sib_z, ring_b, z_b, fin, zr, tot,
                  lm, lz, sm_s, sm_r, sz_s, sz_r, rg_s, rg_r, zz_s, zz_r, c_s, c_r, b_s, b_r, f_s, f_r, t_s):
    o, h, z, core, near, owners = place()
    color = z % 3
    sib = (o, h + 1 - 2 * core)
    zs = [(o, ((z + k) % ZS) * 2 + core) for k in range(ZS)]
    greet([sib] + zs[1:] + near)
    zdev = [zs[ZS - 1], zs[1]]
    pair = [((color + 1) % 3) * PAIR, ((color + 2) % 3) * PAIR]
    miss = [color * PAIR, color * PAIR + SUB]

    def src(n, side, row, count):
        return part.at[pl.ds(pl.multiple_of(owners[n] * ROWS + side * HALF + row, SUB), count)]

    def load_z(p, n):
        return pltpu.make_async_copy(src(n, core, miss[p], SUB), own_z.at[p, n], lz.at[p, n])

    def load_m(p, n):
        return pltpu.make_async_copy(src(n, core, pair[p], PAIR), own_m.at[p, n], lm.at[p, n])

    def give_z(p, n):
        return send(src(n, 1 - core, miss[p], SUB), sib_z.at[p, n], sz_s.at[p], sz_r.at[p, n], sib)

    def give_m(p, n):
        return send(src(n, 1 - core, pair[p], PAIR), sib_m.at[p, n], sm_s.at[p], sm_r.at[p, n], sib)

    def zcopy(p, n):
        return send(own_z.at[p, n], z_b.at[p, n], zz_s.at[p], zz_r.at[p, n], zdev[p])

    def rcopy(p, n, direction):
        return send(own_m.at[p, n], ring_b.at[p, n], rg_s.at[p], rg_r.at[p, n], near[direction ^ 1])

    reached = [{m: d for l in TREES[p] for m, d in l} for p in (0, 1)]

    def fetch(p, n):
        for make in (give_z, load_z, give_m, load_m):
            make(p, n).start()

    def zpart(p, n):
        load_z(p, n).wait()
        give_z(p, n).wait_recv()

        def add(i, _):
            r = pl.ds(pl.multiple_of(i * 128, 128), 128)
            own_z[p, n, r, :] = (own_z[p, n, r, :].astype(jnp.float32) + sib_z[p, n, r, :].astype(jnp.float32)).astype(jnp.bfloat16)
            return 0
        lax.fori_loop(0, SUB // 128, add, 0)
        zcopy(p, n).start()

    def total(p, n):
        load_m(p, n).wait()
        give_m(p, n).wait_recv()
        zcopy(p, n).wait_recv()
        for m, direction in TREES[p][n]:
            rcopy(p, m, direction).wait_recv()

        def add(i, _, with_z, first):
            r = pl.ds(pl.multiple_of(first + i * 128, 128), 128)
            t = own_m[p, n, r, :].astype(jnp.float32) + sib_m[p, n, r, :].astype(jnp.float32)
            if with_z:
                t = t + z_b[p, n, pl.ds(pl.multiple_of(i * 128, 128), 128), :].astype(jnp.float32)
            for m, _direction in TREES[p][n]:
                t = t + ring_b[p, m, r, :].astype(jnp.float32)
            t = t.astype(jnp.bfloat16)
            if n == 0:
                fin[p, r, :] = t
            else:
                own_m[p, n, r, :] = t
            return 0
        lax.fori_loop(0, SUB // 128, lambda i, x: add(i, x, p == 0, 0), 0)
        lax.fori_loop(0, SUB // 128, lambda i, x: add(i, x, p == 1, SUB), 0)
        if n:
            rcopy(p, n, reached[p][n]).start()

    for k in range(-LOAD_AHEAD, len(BACK)):
        if k == -LOAD_AHEAD:
            for e in BACK[:LOAD_AHEAD]:
                fetch(*e)
        if 0 <= k and k + LOAD_AHEAD < len(BACK):
            fetch(*BACK[k + LOAD_AHEAD])
        if -Z_AHEAD <= k and k + Z_AHEAD < len(BACK):
            zpart(*BACK[k + Z_AHEAD])
        if k >= 0:
            total(*BACK[k])

    hops = [3, 6, 9, 1, 4, 7, 10]

    def scatter(k):
        hop = hops[k]
        to = (z + hop) % ZS
        ref = fin.at[0 if k < 3 else 1, pl.ds(pl.multiple_of((to // 3) * CHUNK, CHUNK), CHUNK)]
        return send(ref, zr.at[k], c_s.at[k], c_r.at[k], zs[hop])
    for k in (1, 4, 5, 0, 2, 6, 3):
        scatter(k).start()
    mine = pl.ds(pl.multiple_of((z // 3) * CHUNK, CHUNK), CHUNK)
    for k in range(7):
        scatter(k).wait_recv()
    t = fin[0, mine, :].astype(jnp.float32)
    for k in range(7):
        t = t + zr[k].astype(jnp.float32)
    tot[...] = t.astype(jnp.bfloat16)

    def chunk_rows(layer):
        return out.at[pl.ds(pl.multiple_of(core * HALF + ((layer % 3 + 1) % 3) * PAIR + (layer // 3) * CHUNK, CHUNK), CHUNK)]

    def spread(k):
        return send(tot, chunk_rows(z), b_s.at[k], b_r.at[k], zs[k])

    def arrived(k):
        ref = chunk_rows((z + ZS - k) % ZS)
        return send(ref, ref, f_s.at[k], f_r.at[k], sib)

    far = [6, 5, 7, 4, 8, 3, 9, 2, 10, 1, 11]
    near_first = far[::-1]
    for k in far:
        spread(k).start()
    first = send(tot, chunk_rows(z), f_s.at[0], f_r.at[0], sib)
    first.start()
    keep = pltpu.make_async_copy(tot, chunk_rows(z), t_s)
    keep.start()
    for k in near_first:
        ref = chunk_rows((z + ZS - k) % ZS)
        pltpu.make_async_copy(ref, ref, b_r.at[k]).wait()
        arrived(k).start()
    keep.wait()
    first.wait()
    for k in far:
        spread(k).wait_send()
        arrived(k).wait()
    for k in range(7):
        scatter(k).wait_send()
    for p in (0, 1):
        for ref, sem in (
            (own_z.at[p], sz_s), (own_m.at[p], sm_s), (own_z.at[p], zz_s), (own_m.at[p, pl.ds(1, OWNERS - 1)], rg_s)
        ):
            pltpu.make_async_copy(ref, ref, sem.at[p]).wait()


def reduce_tables(part):
    bf = jnp.bfloat16
    n = OWNERS
    return pl.pallas_call(
        reduce_kernel,
        out_shape=jax.ShapeDtypeStruct((ROWS, 128), bf),
        in_specs=[pl.BlockSpec(memory_space=pl.ANY)],
        out_specs=pl.BlockSpec(memory_space=pl.ANY),
        scratch_shapes=[
            pltpu.VMEM((2, n, PAIR, 128), bf), pltpu.VMEM((2, n, SUB, 128), bf),
            pltpu.VMEM((2, n, PAIR, 128), bf), pltpu.VMEM((2, n, SUB, 128), bf),
            pltpu.VMEM((2, n, PAIR, 128), bf), pltpu.VMEM((2, n, SUB, 128), bf),
            pltpu.VMEM((2, PAIR, 128), bf), pltpu.VMEM((7, CHUNK, 128), bf), pltpu.VMEM((CHUNK, 128), bf),
        ] + [dma(2, n)] * 2 + [dma(2), dma(2, n)] * 4 + [dma(7)] * 2 + [dma(ZS)] * 4 + [dma()],
        compiler_params=pltpu.CompilerParams(collective_id=3, has_side_effects=True, vmem_limit_bytes=56 * 1024 * 1024),
        cost_estimate=pl.CostEstimate(flops=0, bytes_accessed=50000000, transcendentals=0),
        name="reduce_tables",
    )(part)


NT = (((1,), (1,)), ((), ()))


def cross_kernel(dense, fetched, labels, down_hbm, up_hbm, bias, weight, logits, grads, joined, mixed, down, up, sem):
    samples = dense.shape[0]
    take_down = pltpu.make_async_copy(down_hbm, down, sem.at[0])
    take_up = pltpu.make_async_copy(up_hbm, up, sem.at[1])
    take_down.start()
    take_up.start()
    joined[:, 0:128] = dense[...]
    for t in range(26):
        joined[:, 128 * (t + 1):128 * (t + 2)] = fetched[samples * t:samples * (t + 1), :]

    def columns(i, width):
        return pl.ds(pl.multiple_of(i * width, 128), width)

    take_down.wait()

    def first(i, acc):
        c = columns(i, 1152)
        return acc + jnp.dot(joined[:, c], down[c, :], preferred_element_type=jnp.float32)
    lowrank = lax.fori_loop(0, 3, first, jnp.zeros((samples, 512), jnp.float32)).astype(jnp.bfloat16)

    take_up.wait()

    def second(i, acc):
        c = columns(i, 384)
        m = 1.0 + (jnp.dot(lowrank, up[:, c], preferred_element_type=jnp.float32) + bias[:, c])
        mixed[:, c] = m
        v = joined[:, c].astype(jnp.float32) * m * weight[:, c]
        return acc + (v[:, 0:128] + v[:, 128:256] + v[:, 256:384])
    acc = lax.fori_loop(0, 9, second, jnp.zeros((samples, 128), jnp.float32))
    logit = jnp.sum(acc, axis=1, keepdims=True)
    logits[...] = logit
    slope = jax.nn.sigmoid(logit) - labels[...].astype(jnp.float32)

    def third(i, acc):
        c = columns(i, 1152)
        s = (slope * weight[:, c] * joined[:, c].astype(jnp.float32)).astype(jnp.bfloat16)
        return acc + lax.dot_general(s, up[:, c], NT, preferred_element_type=jnp.float32)
    back = lax.fori_loop(0, 3, third, jnp.zeros((samples, 512), jnp.float32)).astype(jnp.bfloat16)

    def fourth(i, _):
        c = pl.ds(pl.multiple_of(128 + i * 256, 128), 256)
        e = slope * weight[:, c] * mixed[:, c] + lax.dot_general(
            back, down[c, :], NT, preferred_element_type=jnp.float32)
        e = e.astype(jnp.bfloat16)
        r = pl.multiple_of(i * 2 * samples, 512)
        grads[pl.ds(r, samples), :] = e[:, 0:128]
        grads[pl.ds(r + samples, samples), :] = e[:, 128:256]
        return 0
    lax.fori_loop(0, 13, fourth, 0)


def cross_layer(dense, fetched, labels, down, up, bias, weight):
    samples = dense.shape[0]
    vmem = pl.BlockSpec(memory_space=pltpu.VMEM)
    return pl.pallas_call(
        cross_kernel,
        out_shape=(
            jax.ShapeDtypeStruct((samples, 1), jnp.float32),
            jax.ShapeDtypeStruct(fetched.shape, jnp.bfloat16)),
        in_specs=[vmem] * 3 + [pl.BlockSpec(memory_space=pl.ANY)] * 2 + [vmem] * 2,
        out_specs=[vmem] * 2,
        scratch_shapes=[pltpu.VMEM((samples, 3456), jnp.bfloat16), pltpu.VMEM((samples, 3456), jnp.float32),
                        pltpu.VMEM(down.shape, jnp.bfloat16), pltpu.VMEM(up.shape, jnp.bfloat16), dma(2)],
        compiler_params=pltpu.CompilerParams(vmem_limit_bytes=60 * 1024 * 1024),
        name="cross_layer",
    )(dense, fetched, labels, down, up, bias, weight)


learn_rate = 0.1


def body(
    dense_input,
    owner_route,
    local_row,
    labels,
    table_rows,
    adagrad_state,
    cross_down,
    cross_up,
    cross_bias,
    out_weight,
):
    samples = dense_input.shape[0]
    tables = local_row.shape[1]
    lookups = samples * tables
    ids = (owner_route.reshape(samples, tables) * ROWS + local_row).T.reshape(lookups)
    fetched = gather_tables(table_rows.astype(jnp.bfloat16))[ids]
    logits, emb_grad = cross_layer(
        dense_input, fetched, labels[:, None], cross_down, cross_up, cross_bias[None, :], out_weight[None, :]
    )
    row_grad = reduce_tables(scatter_rows(ids, emb_grad)).astype(jnp.float32)
    fresh_state = adagrad_state + jnp.mean(row_grad * row_grad, axis=1)
    new_rows = table_rows - learn_rate * row_grad / jnp.sqrt(fresh_state)[:, None]
    return (new_rows, logits.reshape(samples))


def solution(mesh):
    in_specs = (
        P(("owner", "hst"), None),
        P(("owner", "hst"), None, None),
        P(("owner", "hst"), None),
        P(("owner", "hst")),
        P("owner", None),
        P("owner"),
        P(),
        P(),
        P(),
        P(),
    )
    out_specs = (P("owner", None), P(("owner", "hst")))
    return jax.shard_map(body, mesh=mesh, in_specs=in_specs, out_specs=out_specs, check_vma=False)
```

```python
import heapq
import jax
import jax.numpy as jnp
from jax import lax
from jax.experimental import pallas as pl
from jax.experimental.pallas import tpu as pltpu
from jax.sharding import PartitionSpec as P

XS, YS, ZS, OWNERS = 4, 8, 12, 32
ROWS = 3072
HALF, PAIR, SUB = 1536, 512, 256
TABLE = OWNERS * ROWS
STEPS = ((1, 0), (-1, 0), (0, 1), (0, -1))


def trees():
    children = [[[] for _ in range(OWNERS)] for _ in range(2)]

    def grow(plan, parent, direction):
        i, j = parent[0] + STEPS[direction][0], parent[1] + STEPS[direction][1]
        children[plan][parent[0] % XS * YS + parent[1] % YS].append((i % XS * YS + j % YS, direction))
        return i, j

    def line(plan, start, direction, count):
        for _ in range(count):
            start = grow(plan, start, direction)
        return start

    def over_x(plan, start, up):
        line(plan, start, 0, up)
        line(plan, start, 1, 3 - up)

    over_x(0, (0, 0), 2)
    for i in range(XS):
        far = line(0, (i, 0), 2, 4 if i == 0 else 3)
        line(0, (i, 0), 3, 3)
        if i == 0:
            over_x(0, far, 1)
    line(1, (0, 0), 2, 3)
    line(1, (0, 0), 3, 4)
    for j in range(YS):
        over_x(1, (0, j), 2 - j % 2)
    return children


def depths(children, n):
    return 1 + max([depths(children, m) for m, _ in children[n]], default=0)


TIME, DELAY = 2.85, 4.0


def schedule(children):
    waiting, busy, events, steps = [[] for _ in STEPS], [False] * 4, [(0.0, 0, 0, 0), (0.0, 1, 1, 0)], []
    while events:
        now, _, plan, n = heapq.heappop(events)
        if plan < 0:
            busy[n] = False
        else:
            if n:
                steps.append((now, 0, len(steps), (plan, n)))
            for m, direction in children[plan][n]:
                heapq.heappush(waiting[direction], (-depths(children[plan], m), now, len(steps), m, plan, n))
        for direction in range(4):
            if waiting[direction] and not busy[direction]:
                _, ready, _, m, p, parent = heapq.heappop(waiting[direction])
                busy[direction] = True
                steps.append((max(ready, now - TIME), 1, len(steps), (p, parent, m, direction)))
                heapq.heappush(events, (now + TIME, 1000 + direction, -1, direction))
                heapq.heappush(events, (now + TIME + DELAY, 2000 + len(steps), p, m))
    return [step[3] for step in sorted(steps)]


TREES = trees()
SCHEDULE = schedule(TREES)
ORDER = [step for step in SCHEDULE if len(step) == 2]


def place():
    o = lax.axis_index("owner")
    h = lax.axis_index("hst")
    x, y, z, core = o // YS, o % YS, h // 2, h % 2
    near = [(((x + i + XS) % XS) * YS + (y + j + YS) % YS, h) for i, j in STEPS]
    owners = [((x + XS - n // YS) % XS) * YS + (y + YS - n % YS) % YS for n in range(OWNERS)]
    return o, h, z, core, near, owners


def greet(devices):
    barrier = pltpu.get_barrier_semaphore()
    for d in devices:
        pl.semaphore_signal(barrier, inc=1, device_id=d, device_id_type=pl.DeviceIdType.MESH)
    pl.semaphore_wait(barrier, len(devices))


def send(src, dst, ssem, rsem, device):
    return pltpu.make_async_remote_copy(
        src_ref=src, dst_ref=dst, send_sem=ssem, recv_sem=rsem,
        device_id=device, device_id_type=pl.DeviceIdType.MESH)


Z_LAG = 6


def gather_kernel(tab, out, own_sem, ring_s, ring_r, sib_s, sib_r, z_s, z_r, zs_s, zs_r):
    o, h, z, core, near, owners = place()
    color = z % 3
    sib = (o, h + 1 - 2 * core)
    zdev = [(o, ((z + 1) % ZS) * 2 + core), (o, ((z + ZS - 1) % ZS) * 2 + core)]
    greet([sib] + zdev + near)
    base = core * HALF
    pair_row = [base + ((color + 1) % 3) * PAIR, base + ((color + 2) % 3) * PAIR]
    miss_row = [base + color * PAIR, base + color * PAIR + SUB]

    own = pltpu.make_async_copy(tab, out.at[pl.ds(pl.multiple_of(o * ROWS, ROWS), ROWS)], own_sem)
    own.start()

    def rows(n, row, count):
        return out.at[pl.ds(pl.multiple_of(owners[n] * ROWS + row, SUB), count)]

    def ring(p, n, m, direction):
        ref = rows(n, pair_row[p], PAIR)
        src = ref if n else tab.at[pl.ds(pl.multiple_of(pair_row[p], SUB), PAIR)]
        return send(src, ref, ring_s.at[p], ring_r.at[p, m], near[direction])

    def sibling(p, n):
        ref = rows(n, pair_row[p], PAIR)
        return send(ref, ref, sib_s.at[p], sib_r.at[p], sib)

    def zed(p, n):
        ref = rows(n, pair_row[p] + p * SUB, SUB)
        return send(ref, ref, z_s.at[p], z_r.at[p, n], zdev[p])

    def zsib(p, n):
        ref = rows(n, miss_row[p], SUB)
        return send(ref, ref, zs_s.at[p], zs_r.at[p], sib)

    def await_(ref, sem):
        pltpu.make_async_copy(ref, ref, sem).wait()

    def from_z(p, n):
        await_(rows(n, miss_row[p], SUB), z_r.at[p, n])
        zsib(p, n).start()

    came = []
    for step in SCHEDULE:
        if len(step) == 4:
            ring(*step).start()
            continue
        p, n = step
        await_(rows(n, pair_row[p], PAIR), ring_r.at[p, n])
        came.append(step)
        zed(p, n).start()
        sibling(p, n).start()
        if len(came) > Z_LAG:
            from_z(*came[-1 - Z_LAG])
    for step in came[-Z_LAG:]:
        from_z(*step)
    whole, half = out.at[pl.ds(0, 31 * PAIR)], out.at[pl.ds(0, 31 * SUB)]
    for p in (0, 1):
        await_(whole, sib_r.at[p])
        await_(half, zs_r.at[p])
        for sem in (ring_s, sib_s):
            await_(whole, sem.at[p])
        for sem in (z_s, zs_s):
            await_(half, sem.at[p])
    own.wait()


def dma(*shape):
    return pltpu.SemaphoreType.DMA(shape)


def gather_tables(tab):
    return pl.pallas_call(
        gather_kernel,
        out_shape=jax.ShapeDtypeStruct((TABLE, 128), jnp.bfloat16),
        in_specs=[pl.BlockSpec(memory_space=pl.ANY)],
        out_specs=pl.BlockSpec(memory_space=pl.ANY),
        scratch_shapes=[dma()] + [dma(2), dma(2, OWNERS), dma(2), dma(2), dma(2), dma(2, OWNERS), dma(2), dma(2)],
        compiler_params=pltpu.CompilerParams(collective_id=2, has_side_effects=True),
        cost_estimate=pl.CostEstimate(flops=0, bytes_accessed=50000000, transcendentals=0),
        name="gather_tables",
    )(tab)


LOOKUPS = 6656


def scatter_kernel(ids, g, out, acc, gf, stage, sem):
    def clear(i, _):
        acc[pl.ds(pl.multiple_of(i * 1024, 1024), 1024), :] = jnp.zeros((1024, 128), jnp.float32)
        return 0
    lax.fori_loop(0, TABLE // 1024, clear, 0)

    def widen(i, _):
        r = pl.ds(pl.multiple_of(i * 128, 128), 128)
        gf[r, :] = g[r, :].astype(jnp.float32)
        return 0
    lax.fori_loop(0, LOOKUPS // 128, widen, 0)

    def add(i, _):
        for k in range(16):
            j = i * 16 + k
            row = ids[j]
            acc[pl.ds(row, 1), :] = acc[pl.ds(row, 1), :] + gf[pl.ds(j, 1), :]
        return 0
    lax.fori_loop(0, LOOKUPS // 16, add, 0)

    def copy(i):
        slot = i % 2
        return pltpu.make_async_copy(stage.at[slot], out.at[pl.ds(pl.multiple_of(i * ROWS, ROWS), ROWS)], sem.at[slot])

    def write(i, _):
        @pl.when(i >= 2)
        def _():
            copy(i - 2).wait()

        def narrow(k, _):
            r = pl.multiple_of(k * 512, 512)
            stage[i % 2, pl.ds(r, 512), :] = acc[pl.ds(pl.multiple_of(i * ROWS + r, 512), 512), :].astype(jnp.bfloat16)
            return 0
        lax.fori_loop(0, ROWS // 512, narrow, 0)
        copy(i).start()
        return 0
    lax.fori_loop(0, OWNERS, write, 0)
    copy(OWNERS - 2).wait()
    copy(OWNERS - 1).wait()


def scatter_rows(ids, g):
    return pl.pallas_call(
        scatter_kernel,
        out_shape=jax.ShapeDtypeStruct((TABLE, 128), jnp.bfloat16),
        in_specs=[pl.BlockSpec(memory_space=pltpu.SMEM), pl.BlockSpec(memory_space=pltpu.VMEM)],
        out_specs=pl.BlockSpec(memory_space=pl.ANY),
        scratch_shapes=[
            pltpu.VMEM((TABLE, 128), jnp.float32), pltpu.VMEM((LOOKUPS, 128), jnp.float32),
            pltpu.VMEM((2, ROWS, 128), jnp.bfloat16), pltpu.SemaphoreType.DMA((2,))],
        compiler_params=pltpu.CompilerParams(vmem_limit_bytes=60 * 1024 * 1024),
        name="scatter_rows",
    )(ids, g)


CHUNK = 128
LOAD_AHEAD, Z_AHEAD = 20, 10
BACK = [e for e in reversed(ORDER)] + [(0, 0), (1, 0)]


def reduce_kernel(part, out, own_m, own_z, sib_m, sib_z, ring_b, z_b, fin, zr, tot,
                  lm, lz, sm_s, sm_r, sz_s, sz_r, rg_s, rg_r, zz_s, zz_r, c_s, c_r, b_s, b_r, f_s, f_r, t_s):
    o, h, z, core, near, owners = place()
    color = z % 3
    sib = (o, h + 1 - 2 * core)
    zs = [(o, ((z + k) % ZS) * 2 + core) for k in range(ZS)]
    greet([sib] + zs[1:] + near)
    zdev = [zs[ZS - 1], zs[1]]
    pair = [((color + 1) % 3) * PAIR, ((color + 2) % 3) * PAIR]
    miss = [color * PAIR, color * PAIR + SUB]

    def src(n, side, row, count):
        return part.at[pl.ds(pl.multiple_of(owners[n] * ROWS + side * HALF + row, SUB), count)]

    def load_z(p, n):
        return pltpu.make_async_copy(src(n, core, miss[p], SUB), own_z.at[p, n], lz.at[p, n])

    def load_m(p, n):
        return pltpu.make_async_copy(src(n, core, pair[p], PAIR), own_m.at[p, n], lm.at[p, n])

    def give_z(p, n):
        return send(src(n, 1 - core, miss[p], SUB), sib_z.at[p, n], sz_s.at[p], sz_r.at[p, n], sib)

    def give_m(p, n):
        return send(src(n, 1 - core, pair[p], PAIR), sib_m.at[p, n], sm_s.at[p], sm_r.at[p, n], sib)

    def zcopy(p, n):
        return send(own_z.at[p, n], z_b.at[p, n], zz_s.at[p], zz_r.at[p, n], zdev[p])

    def rcopy(p, n, direction):
        return send(own_m.at[p, n], ring_b.at[p, n], rg_s.at[p], rg_r.at[p, n], near[direction ^ 1])

    reached = [{m: d for l in TREES[p] for m, d in l} for p in (0, 1)]

    def fetch(p, n):
        for make in (give_z, load_z, give_m, load_m):
            make(p, n).start()

    def zpart(p, n):
        load_z(p, n).wait()
        give_z(p, n).wait_recv()

        def add(i, _):
            r = pl.ds(pl.multiple_of(i * 128, 128), 128)
            own_z[p, n, r, :] = (own_z[p, n, r, :].astype(jnp.float32) + sib_z[p, n, r, :].astype(jnp.float32)).astype(jnp.bfloat16)
            return 0
        lax.fori_loop(0, SUB // 128, add, 0)
        zcopy(p, n).start()

    def total(p, n):
        load_m(p, n).wait()
        give_m(p, n).wait_recv()
        zcopy(p, n).wait_recv()
        for m, direction in TREES[p][n]:
            rcopy(p, m, direction).wait_recv()

        def add(i, _, with_z, first):
            r = pl.ds(pl.multiple_of(first + i * 128, 128), 128)
            t = own_m[p, n, r, :].astype(jnp.float32) + sib_m[p, n, r, :].astype(jnp.float32)
            if with_z:
                t = t + z_b[p, n, pl.ds(pl.multiple_of(i * 128, 128), 128), :].astype(jnp.float32)
            for m, _direction in TREES[p][n]:
                t = t + ring_b[p, m, r, :].astype(jnp.float32)
            t = t.astype(jnp.bfloat16)
            if n == 0:
                fin[p, r, :] = t
            else:
                own_m[p, n, r, :] = t
            return 0
        lax.fori_loop(0, SUB // 128, lambda i, x: add(i, x, p == 0, 0), 0)
        lax.fori_loop(0, SUB // 128, lambda i, x: add(i, x, p == 1, SUB), 0)
        if n:
            rcopy(p, n, reached[p][n]).start()

    for k in range(-LOAD_AHEAD, len(BACK)):
        if k == -LOAD_AHEAD:
            for e in BACK[:LOAD_AHEAD]:
                fetch(*e)
        if 0 <= k and k + LOAD_AHEAD < len(BACK):
            fetch(*BACK[k + LOAD_AHEAD])
        if -Z_AHEAD <= k and k + Z_AHEAD < len(BACK):
            zpart(*BACK[k + Z_AHEAD])
        if k >= 0:
            total(*BACK[k])

    hops = [3, 6, 9, 1, 4, 7, 10]

    def scatter(k):
        hop = hops[k]
        to = (z + hop) % ZS
        ref = fin.at[0 if k < 3 else 1, pl.ds(pl.multiple_of((to // 3) * CHUNK, CHUNK), CHUNK)]
        return send(ref, zr.at[k], c_s.at[k], c_r.at[k], zs[hop])
    for k in (1, 4, 5, 0, 2, 6, 3):
        scatter(k).start()
    mine = pl.ds(pl.multiple_of((z // 3) * CHUNK, CHUNK), CHUNK)
    for k in range(7):
        scatter(k).wait_recv()
    t = fin[0, mine, :].astype(jnp.float32)
    for k in range(7):
        t = t + zr[k].astype(jnp.float32)
    tot[...] = t.astype(jnp.bfloat16)

    def chunk_rows(layer):
        return out.at[pl.ds(pl.multiple_of(core * HALF + ((layer % 3 + 1) % 3) * PAIR + (layer // 3) * CHUNK, CHUNK), CHUNK)]

    def spread(k):
        return send(tot, chunk_rows(z), b_s.at[k], b_r.at[k], zs[k])

    def arrived(k):
        ref = chunk_rows((z + ZS - k) % ZS)
        return send(ref, ref, f_s.at[k], f_r.at[k], sib)

    far = [6, 5, 7, 4, 8, 3, 9, 2, 10, 1, 11]
    near_first = far[::-1]
    for k in far:
        spread(k).start()
    first = send(tot, chunk_rows(z), f_s.at[0], f_r.at[0], sib)
    first.start()
    keep = pltpu.make_async_copy(tot, chunk_rows(z), t_s)
    keep.start()
    for k in near_first:
        ref = chunk_rows((z + ZS - k) % ZS)
        pltpu.make_async_copy(ref, ref, b_r.at[k]).wait()
        arrived(k).start()
    keep.wait()
    first.wait()
    for k in far:
        spread(k).wait_send()
        arrived(k).wait()
    for k in range(7):
        scatter(k).wait_send()
    for p in (0, 1):
        for ref, sem in (
            (own_z.at[p], sz_s), (own_m.at[p], sm_s), (own_z.at[p], zz_s), (own_m.at[p, pl.ds(1, OWNERS - 1)], rg_s)
        ):
            pltpu.make_async_copy(ref, ref, sem.at[p]).wait()


def reduce_tables(part):
    bf = jnp.bfloat16
    n = OWNERS
    return pl.pallas_call(
        reduce_kernel,
        out_shape=jax.ShapeDtypeStruct((ROWS, 128), bf),
        in_specs=[pl.BlockSpec(memory_space=pl.ANY)],
        out_specs=pl.BlockSpec(memory_space=pl.ANY),
        scratch_shapes=[
            pltpu.VMEM((2, n, PAIR, 128), bf), pltpu.VMEM((2, n, SUB, 128), bf),
            pltpu.VMEM((2, n, PAIR, 128), bf), pltpu.VMEM((2, n, SUB, 128), bf),
            pltpu.VMEM((2, n, PAIR, 128), bf), pltpu.VMEM((2, n, SUB, 128), bf),
            pltpu.VMEM((2, PAIR, 128), bf), pltpu.VMEM((7, CHUNK, 128), bf), pltpu.VMEM((CHUNK, 128), bf),
        ] + [dma(2, n)] * 2 + [dma(2), dma(2, n)] * 4 + [dma(7)] * 2 + [dma(ZS)] * 4 + [dma()],
        compiler_params=pltpu.CompilerParams(collective_id=3, has_side_effects=True, vmem_limit_bytes=56 * 1024 * 1024),
        cost_estimate=pl.CostEstimate(flops=0, bytes_accessed=50000000, transcendentals=0),
        name="reduce_tables",
    )(part)


NT = (((1,), (1,)), ((), ()))


def cross_kernel(dense, fetched, labels, down_hbm, up_hbm, bias, weight, logits, grads, joined, mixed, down, up, sem):
    samples = dense.shape[0]
    take_down = pltpu.make_async_copy(down_hbm, down, sem.at[0])
    take_up = pltpu.make_async_copy(up_hbm, up, sem.at[1])
    take_down.start()
    take_up.start()
    joined[:, 0:128] = dense[...]
    for t in range(26):
        joined[:, 128 * (t + 1):128 * (t + 2)] = fetched[samples * t:samples * (t + 1), :]

    def columns(i, width):
        return pl.ds(pl.multiple_of(i * width, 128), width)

    take_down.wait()

    def first(i, acc):
        c = columns(i, 1152)
        return acc + jnp.dot(joined[:, c], down[c, :], preferred_element_type=jnp.float32)
    lowrank = lax.fori_loop(0, 3, first, jnp.zeros((samples, 512), jnp.float32)).astype(jnp.bfloat16)

    take_up.wait()

    def second(i, acc):
        c = columns(i, 384)
        m = 1.0 + (jnp.dot(lowrank, up[:, c], preferred_element_type=jnp.float32) + bias[:, c])
        mixed[:, c] = m
        v = joined[:, c].astype(jnp.float32) * m * weight[:, c]
        return acc + (v[:, 0:128] + v[:, 128:256] + v[:, 256:384])
    acc = lax.fori_loop(0, 9, second, jnp.zeros((samples, 128), jnp.float32))
    logit = jnp.sum(acc, axis=1, keepdims=True)
    logits[...] = logit
    slope = jax.nn.sigmoid(logit) - labels[...].astype(jnp.float32)

    def third(i, acc):
        c = columns(i, 1152)
        s = (slope * weight[:, c] * joined[:, c].astype(jnp.float32)).astype(jnp.bfloat16)
        return acc + lax.dot_general(s, up[:, c], NT, preferred_element_type=jnp.float32)
    back = lax.fori_loop(0, 3, third, jnp.zeros((samples, 512), jnp.float32)).astype(jnp.bfloat16)

    def fourth(i, _):
        c = pl.ds(pl.multiple_of(128 + i * 256, 128), 256)
        e = slope * weight[:, c] * mixed[:, c] + lax.dot_general(
            back, down[c, :], NT, preferred_element_type=jnp.float32)
        e = e.astype(jnp.bfloat16)
        r = pl.multiple_of(i * 2 * samples, 512)
        grads[pl.ds(r, samples), :] = e[:, 0:128]
        grads[pl.ds(r + samples, samples), :] = e[:, 128:256]
        return 0
    lax.fori_loop(0, 13, fourth, 0)


def cross_layer(dense, fetched, labels, down, up, bias, weight):
    samples = dense.shape[0]
    vmem = pl.BlockSpec(memory_space=pltpu.VMEM)
    return pl.pallas_call(
        cross_kernel,
        out_shape=(
            jax.ShapeDtypeStruct((samples, 1), jnp.float32),
            jax.ShapeDtypeStruct(fetched.shape, jnp.bfloat16)),
        in_specs=[vmem] * 3 + [pl.BlockSpec(memory_space=pl.ANY)] * 2 + [vmem] * 2,
        out_specs=[vmem] * 2,
        scratch_shapes=[pltpu.VMEM((samples, 3456), jnp.bfloat16), pltpu.VMEM((samples, 3456), jnp.float32),
                        pltpu.VMEM(down.shape, jnp.bfloat16), pltpu.VMEM(up.shape, jnp.bfloat16), dma(2)],
        compiler_params=pltpu.CompilerParams(vmem_limit_bytes=60 * 1024 * 1024),
        name="cross_layer",
    )(dense, fetched, labels, down, up, bias, weight)


learn_rate = 0.1


def body(
    dense_input,
    owner_route,
    local_row,
    labels,
    table_rows,
    adagrad_state,
    cross_down,
    cross_up,
    cross_bias,
    out_weight,
):
    samples = dense_input.shape[0]
    tables = local_row.shape[1]
    lookups = samples * tables
    ids = (owner_route.reshape(samples, tables) * ROWS + local_row).T.reshape(lookups)
    fetched = gather_tables(table_rows.astype(jnp.bfloat16))[ids]
    logits, emb_grad = cross_layer(
        dense_input, fetched, labels[:, None], cross_down, cross_up, cross_bias[None, :], out_weight[None, :]
    )
    row_grad = reduce_tables(scatter_rows(ids, emb_grad)).astype(jnp.float32)
    fresh_state = adagrad_state + jnp.mean(row_grad * row_grad, axis=1)
    new_rows = table_rows - learn_rate * row_grad / jnp.sqrt(fresh_state)[:, None]
    return (new_rows, logits.reshape(samples))


def solution(mesh):
    in_specs = (
        P(("owner", "hst"), None),
        P(("owner", "hst"), None, None),
        P(("owner", "hst"), None),
        P(("owner", "hst")),
        P("owner", None),
        P("owner"),
        P(),
        P(),
        P(),
        P(),
    )
    out_specs = (P("owner", None), P(("owner", "hst")))
    return jax.shard_map(body, mesh=mesh, in_specs=in_specs, out_specs=out_specs, check_vma=False)
```

```python
import heapq
import jax
import jax.numpy as jnp
from jax import lax
from jax.experimental import pallas as pl
from jax.experimental.pallas import tpu as pltpu
from jax.sharding import PartitionSpec as P

XS, YS, ZS, OWNERS = 4, 8, 12, 32
ROWS = 3072
HALF, PAIR, SUB = 1536, 512, 256
TABLE = OWNERS * ROWS
STEPS = ((1, 0), (-1, 0), (0, 1), (0, -1))


def trees():
    children = [[[] for _ in range(OWNERS)] for _ in range(2)]

    def grow(plan, parent, direction):
        i, j = parent[0] + STEPS[direction][0], parent[1] + STEPS[direction][1]
        children[plan][parent[0] % XS * YS + parent[1] % YS].append((i % XS * YS + j % YS, direction))
        return i, j

    def line(plan, start, direction, count):
        for _ in range(count):
            start = grow(plan, start, direction)
        return start

    def over_x(plan, start, up):
        line(plan, start, 0, up)
        line(plan, start, 1, 3 - up)

    over_x(0, (0, 0), 2)
    for i in range(XS):
        far = line(0, (i, 0), 2, 4 if i == 0 else 3)
        line(0, (i, 0), 3, 3)
        if i == 0:
            over_x(0, far, 1)
    line(1, (0, 0), 2, 3)
    line(1, (0, 0), 3, 4)
    for j in range(YS):
        over_x(1, (0, j), 2 - j % 2)
    return children


def depths(children, n):
    return 1 + max([depths(children, m) for m, _ in children[n]], default=0)


TIME, DELAY = 2.85, 4.0


def schedule(children):
    waiting, busy, events, steps = [[] for _ in STEPS], [False] * 4, [(0.0, 0, 0, 0), (0.0, 1, 1, 0)], []
    while events:
        now, _, plan, n = heapq.heappop(events)
        if plan < 0:
            busy[n] = False
        else:
            if n:
                steps.append((now, 0, len(steps), (plan, n)))
            for m, direction in children[plan][n]:
                heapq.heappush(waiting[direction], (-depths(children[plan], m), now, len(steps), m, plan, n))
        for direction in range(4):
            if waiting[direction] and not busy[direction]:
                _, ready, _, m, p, parent = heapq.heappop(waiting[direction])
                busy[direction] = True
                steps.append((max(ready, now - TIME), 1, len(steps), (p, parent, m, direction)))
                heapq.heappush(events, (now + TIME, 1000 + direction, -1, direction))
                heapq.heappush(events, (now + TIME + DELAY, 2000 + len(steps), p, m))
    return [step[3] for step in sorted(steps)]


TREES = trees()
SCHEDULE = schedule(TREES)
ORDER = [step for step in SCHEDULE if len(step) == 2]


def place():
    o = lax.axis_index("owner")
    h = lax.axis_index("hst")
    x, y, z, core = o // YS, o % YS, h // 2, h % 2
    near = [(((x + i + XS) % XS) * YS + (y + j + YS) % YS, h) for i, j in STEPS]
    owners = [((x + XS - n // YS) % XS) * YS + (y + YS - n % YS) % YS for n in range(OWNERS)]
    return o, h, z, core, near, owners


def greet(devices):
    barrier = pltpu.get_barrier_semaphore()
    for d in devices:
        pl.semaphore_signal(barrier, inc=1, device_id=d, device_id_type=pl.DeviceIdType.MESH)
    pl.semaphore_wait(barrier, len(devices))


def send(src, dst, ssem, rsem, device):
    return pltpu.make_async_remote_copy(
        src_ref=src, dst_ref=dst, send_sem=ssem, recv_sem=rsem,
        device_id=device, device_id_type=pl.DeviceIdType.MESH)


Z_LAG = 14


def gather_kernel(tab, out, own_sem, ring_s, ring_r, sib_s, sib_r, z_s, z_r, zs_s, zs_r):
    o, h, z, core, near, owners = place()
    color = z % 3
    sib = (o, h + 1 - 2 * core)
    zdev = [(o, ((z + 1) % ZS) * 2 + core), (o, ((z + ZS - 1) % ZS) * 2 + core)]
    greet([sib] + zdev + near)
    base = core * HALF
    pair_row = [base + ((color + 1) % 3) * PAIR, base + ((color + 2) % 3) * PAIR]
    miss_row = [base + color * PAIR, base + color * PAIR + SUB]

    own = pltpu.make_async_copy(tab, out.at[pl.ds(pl.multiple_of(o * ROWS, ROWS), ROWS)], own_sem)
    own.start()

    def rows(n, row, count):
        return out.at[pl.ds(pl.multiple_of(owners[n] * ROWS + row, SUB), count)]

    def ring(p, n, m, direction):
        ref = rows(n, pair_row[p], PAIR)
        src = ref if n else tab.at[pl.ds(pl.multiple_of(pair_row[p], SUB), PAIR)]
        return send(src, ref, ring_s.at[p], ring_r.at[p, m], near[direction])

    def sibling(p, n):
        ref = rows(n, pair_row[p], PAIR)
        return send(ref, ref, sib_s.at[p], sib_r.at[p], sib)

    def zed(p, n):
        ref = rows(n, pair_row[p] + p * SUB, SUB)
        return send(ref, ref, z_s.at[p], z_r.at[p, n], zdev[p])

    def zsib(p, n):
        ref = rows(n, miss_row[p], SUB)
        return send(ref, ref, zs_s.at[p], zs_r.at[p], sib)

    def await_(ref, sem):
        pltpu.make_async_copy(ref, ref, sem).wait()

    def from_z(p, n):
        await_(rows(n, miss_row[p], SUB), z_r.at[p, n])
        zsib(p, n).start()

    came = []
    for step in SCHEDULE:
        if len(step) == 4:
            ring(*step).start()
            continue
        p, n = step
        await_(rows(n, pair_row[p], PAIR), ring_r.at[p, n])
        came.append(step)
        zed(p, n).start()
        sibling(p, n).start()
        if len(came) > Z_LAG:
            from_z(*came[-1 - Z_LAG])
    for step in came[-Z_LAG:]:
        from_z(*step)
    whole, half = out.at[pl.ds(0, 31 * PAIR)], out.at[pl.ds(0, 31 * SUB)]
    for p in (0, 1):
        await_(whole, sib_r.at[p])
        await_(half, zs_r.at[p])
        for sem in (ring_s, sib_s):
            await_(whole, sem.at[p])
        for sem in (z_s, zs_s):
            await_(half, sem.at[p])
    own.wait()


def dma(*shape):
    return pltpu.SemaphoreType.DMA(shape)


def gather_tables(tab):
    return pl.pallas_call(
        gather_kernel,
        out_shape=jax.ShapeDtypeStruct((TABLE, 128), jnp.bfloat16),
        in_specs=[pl.BlockSpec(memory_space=pl.ANY)],
        out_specs=pl.BlockSpec(memory_space=pl.ANY),
        scratch_shapes=[dma()] + [dma(2), dma(2, OWNERS), dma(2), dma(2), dma(2), dma(2, OWNERS), dma(2), dma(2)],
        compiler_params=pltpu.CompilerParams(collective_id=2, has_side_effects=True),
        cost_estimate=pl.CostEstimate(flops=0, bytes_accessed=50000000, transcendentals=0),
        name="gather_tables",
    )(tab)


NT = (((1,), (1,)), ((), ()))
LOOKUPS, TABLES, SAMPLES, FEAT, RANK = 6656, 26, 256, 3456, 512
WRITE = 1024


def cross_kernel(ids, dense, fetched, labels, down_hbm, up_hbm, bias, weight, logits, out,
                 acc, rows, stage, joined, mixed, down, up, sem, row_sem, out_sem):
    take_down = pltpu.make_async_copy(down_hbm, down, sem.at[0])
    take_up = pltpu.make_async_copy(up_hbm, up, sem.at[1])

    def take_rows(t):
        return pltpu.make_async_copy(
            fetched.at[pl.ds(SAMPLES * t, SAMPLES)], joined.at[:, pl.ds(128 * (t + 1), 128)], row_sem.at[t])
    for t in range(TABLES):
        take_rows(t).start()
    take_down.start()
    take_up.start()
    joined[:, 0:128] = dense[...]

    def clear(i, _):
        acc[pl.ds(pl.multiple_of(i * 1024, 1024), 1024), :] = jnp.zeros((1024, 128), jnp.float32)
        return 0
    lax.fori_loop(0, TABLE // 1024, clear, 0)
    for t in range(TABLES):
        take_rows(t).wait()
    take_down.wait()

    def columns(i, width):
        return pl.ds(pl.multiple_of(i * width, 128), width)

    def first(i, total):
        c = columns(i, 1152)
        return total + jnp.dot(joined[:, c], down[c, :], preferred_element_type=jnp.float32)
    lowrank = lax.fori_loop(0, 3, first, jnp.zeros((SAMPLES, RANK), jnp.float32)).astype(jnp.bfloat16)
    take_up.wait()

    def second(i, total):
        c = columns(i, 384)
        m = 1.0 + (jnp.dot(lowrank, up[:, c], preferred_element_type=jnp.float32) + bias[:, c])
        mixed[:, c] = m
        v = joined[:, c].astype(jnp.float32) * m * weight[:, c]
        return total + (v[:, 0:128] + v[:, 128:256] + v[:, 256:384])
    total = lax.fori_loop(0, 9, second, jnp.zeros((SAMPLES, 128), jnp.float32))
    logit = jnp.sum(total, axis=1, keepdims=True)
    logits[...] = logit
    slope = jax.nn.sigmoid(logit) - labels[...].astype(jnp.float32)

    def third(i, total):
        c = columns(i, 1152)
        s = (slope * weight[:, c] * joined[:, c].astype(jnp.float32)).astype(jnp.bfloat16)
        return total + lax.dot_general(s, up[:, c], NT, preferred_element_type=jnp.float32)
    back = lax.fori_loop(0, 3, third, jnp.zeros((SAMPLES, RANK), jnp.float32)).astype(jnp.bfloat16)

    def fourth(i, _):
        c = pl.ds(pl.multiple_of(128 + i * 256, 128), 256)
        e = slope * weight[:, c] * mixed[:, c] + lax.dot_general(
            back, down[c, :], NT, preferred_element_type=jnp.float32)
        e = e.astype(jnp.bfloat16).astype(jnp.float32)
        rows[0:SAMPLES, :] = e[:, 0:128]
        rows[SAMPLES:2 * SAMPLES, :] = e[:, 128:256]

        def add(k, _):
            for m in range(16):
                j = k * 16 + m
                row = ids[i * (2 * SAMPLES) + j]
                acc[pl.ds(row, 1), :] = acc[pl.ds(row, 1), :] + rows[pl.ds(j, 1), :]
            return 0
        lax.fori_loop(0, 2 * SAMPLES // 16, add, 0)
        return 0
    lax.fori_loop(0, TABLES // 2, fourth, 0)

    def copy(i):
        return pltpu.make_async_copy(
            stage.at[i % 2], out.at[pl.ds(pl.multiple_of(i * WRITE, WRITE), WRITE)], out_sem.at[i % 2])

    def write(i, _):
        @pl.when(i >= 2)
        def _():
            copy(i - 2).wait()

        def narrow(k, _):
            r = pl.multiple_of(k * 512, 512)
            stage[i % 2, pl.ds(r, 512), :] = acc[pl.ds(pl.multiple_of(i * WRITE + r, 512), 512), :].astype(jnp.bfloat16)
            return 0
        lax.fori_loop(0, WRITE // 512, narrow, 0)
        copy(i).start()
        return 0
    lax.fori_loop(0, TABLE // WRITE, write, 0)
    copy(TABLE // WRITE - 2).wait()
    copy(TABLE // WRITE - 1).wait()


def cross_layer(ids, dense, fetched, labels, down, up, bias, weight):
    vmem, hbm = pl.BlockSpec(memory_space=pltpu.VMEM), pl.BlockSpec(memory_space=pl.ANY)
    f32, bf = jnp.float32, jnp.bfloat16
    return pl.pallas_call(
        cross_kernel,
        out_shape=(jax.ShapeDtypeStruct((SAMPLES, 1), f32), jax.ShapeDtypeStruct((TABLE, 128), bf)),
        in_specs=[pl.BlockSpec(memory_space=pltpu.SMEM), vmem, hbm, vmem, hbm, hbm, vmem, vmem],
        out_specs=[vmem, hbm],
        scratch_shapes=[
            pltpu.VMEM((TABLE, 128), f32), pltpu.VMEM((2 * SAMPLES, 128), f32), pltpu.VMEM((2, WRITE, 128), bf),
            pltpu.VMEM((SAMPLES, FEAT), bf), pltpu.VMEM((SAMPLES, FEAT), f32),
            pltpu.VMEM((FEAT, RANK), bf), pltpu.VMEM((RANK, FEAT), bf),
            dma(2), dma(TABLES), dma(2)],
        compiler_params=pltpu.CompilerParams(vmem_limit_bytes=63 * 1024 * 1024),
        name="cross_layer",
    )(ids, dense, fetched, labels, down, up, bias, weight)


CHUNK = 128
LOAD_AHEAD, Z_AHEAD = 20, 10
BACK = [e for e in reversed(ORDER)] + [(0, 0), (1, 0)]


def reduce_kernel(part, out, own_m, own_z, sib_m, sib_z, ring_b, z_b, fin, zr, tot,
                  lm, lz, sm_s, sm_r, sz_s, sz_r, rg_s, rg_r, zz_s, zz_r, c_s, c_r, b_s, b_r, f_s, f_r, t_s):
    o, h, z, core, near, owners = place()
    color = z % 3
    sib = (o, h + 1 - 2 * core)
    zs = [(o, ((z + k) % ZS) * 2 + core) for k in range(ZS)]
    greet([sib] + zs[1:] + near)
    zdev = [zs[ZS - 1], zs[1]]
    pair = [((color + 1) % 3) * PAIR, ((color + 2) % 3) * PAIR]
    miss = [color * PAIR, color * PAIR + SUB]

    def src(n, side, row, count):
        return part.at[pl.ds(pl.multiple_of(owners[n] * ROWS + side * HALF + row, SUB), count)]

    def load_z(p, n):
        return pltpu.make_async_copy(src(n, core, miss[p], SUB), own_z.at[p, n], lz.at[p, n])

    def load_m(p, n):
        return pltpu.make_async_copy(src(n, core, pair[p], PAIR), own_m.at[p, n], lm.at[p, n])

    def give_z(p, n):
        return send(src(n, 1 - core, miss[p], SUB), sib_z.at[p, n], sz_s.at[p], sz_r.at[p, n], sib)

    def give_m(p, n):
        return send(src(n, 1 - core, pair[p], PAIR), sib_m.at[p, n], sm_s.at[p], sm_r.at[p, n], sib)

    def zcopy(p, n):
        return send(own_z.at[p, n], z_b.at[p, n], zz_s.at[p], zz_r.at[p, n], zdev[p])

    def rcopy(p, n, direction):
        return send(own_m.at[p, n], ring_b.at[p, n], rg_s.at[p], rg_r.at[p, n], near[direction ^ 1])

    reached = [{m: d for l in TREES[p] for m, d in l} for p in (0, 1)]

    def fetch(p, n):
        for make in (give_z, load_z, give_m, load_m):
            make(p, n).start()

    def zpart(p, n):
        load_z(p, n).wait()
        give_z(p, n).wait_recv()

        def add(i, _):
            r = pl.ds(pl.multiple_of(i * 128, 128), 128)
            own_z[p, n, r, :] = (own_z[p, n, r, :].astype(jnp.float32) + sib_z[p, n, r, :].astype(jnp.float32)).astype(jnp.bfloat16)
            return 0
        lax.fori_loop(0, SUB // 128, add, 0)
        zcopy(p, n).start()

    def total(p, n):
        load_m(p, n).wait()
        give_m(p, n).wait_recv()
        zcopy(p, n).wait_recv()
        for m, direction in TREES[p][n]:
            rcopy(p, m, direction).wait_recv()

        def add(i, _, with_z, first):
            r = pl.ds(pl.multiple_of(first + i * 128, 128), 128)
            t = own_m[p, n, r, :].astype(jnp.float32) + sib_m[p, n, r, :].astype(jnp.float32)
            if with_z:
                t = t + z_b[p, n, pl.ds(pl.multiple_of(i * 128, 128), 128), :].astype(jnp.float32)
            for m, _direction in TREES[p][n]:
                t = t + ring_b[p, m, r, :].astype(jnp.float32)
            t = t.astype(jnp.bfloat16)
            if n == 0:
                fin[p, r, :] = t
            else:
                own_m[p, n, r, :] = t
            return 0
        lax.fori_loop(0, SUB // 128, lambda i, x: add(i, x, p == 0, 0), 0)
        lax.fori_loop(0, SUB // 128, lambda i, x: add(i, x, p == 1, SUB), 0)
        if n:
            rcopy(p, n, reached[p][n]).start()

    for k in range(-LOAD_AHEAD, len(BACK)):
        if k == -LOAD_AHEAD:
            for e in BACK[:LOAD_AHEAD]:
                fetch(*e)
        if 0 <= k and k + LOAD_AHEAD < len(BACK):
            fetch(*BACK[k + LOAD_AHEAD])
        if -Z_AHEAD <= k and k + Z_AHEAD < len(BACK):
            zpart(*BACK[k + Z_AHEAD])
        if k >= 0:
            total(*BACK[k])

    hops = [3, 6, 9, 1, 4, 7, 10]

    def scatter(k):
        hop = hops[k]
        to = (z + hop) % ZS
        ref = fin.at[0 if k < 3 else 1, pl.ds(pl.multiple_of((to // 3) * CHUNK, CHUNK), CHUNK)]
        return send(ref, zr.at[k], c_s.at[k], c_r.at[k], zs[hop])
    for k in (1, 4, 5, 0, 2, 6, 3):
        scatter(k).start()
    mine = pl.ds(pl.multiple_of((z // 3) * CHUNK, CHUNK), CHUNK)
    for k in range(7):
        scatter(k).wait_recv()
    t = fin[0, mine, :].astype(jnp.float32)
    for k in range(7):
        t = t + zr[k].astype(jnp.float32)
    tot[...] = t.astype(jnp.bfloat16)

    def chunk_rows(layer):
        return out.at[pl.ds(pl.multiple_of(core * HALF + ((layer % 3 + 1) % 3) * PAIR + (layer // 3) * CHUNK, CHUNK), CHUNK)]

    def spread(k):
        return send(tot, chunk_rows(z), b_s.at[k], b_r.at[k], zs[k])

    def arrived(k):
        ref = chunk_rows((z + ZS - k) % ZS)
        return send(ref, ref, f_s.at[k], f_r.at[k], sib)

    far = [6, 5, 7, 4, 8, 3, 9, 2, 10, 1, 11]
    near_first = far[::-1]
    for k in far:
        spread(k).start()
    first = send(tot, chunk_rows(z), f_s.at[0], f_r.at[0], sib)
    first.start()
    keep = pltpu.make_async_copy(tot, chunk_rows(z), t_s)
    keep.start()
    for k in near_first:
        ref = chunk_rows((z + ZS - k) % ZS)
        pltpu.make_async_copy(ref, ref, b_r.at[k]).wait()
        arrived(k).start()
    keep.wait()
    first.wait()
    for k in far:
        spread(k).wait_send()
        arrived(k).wait()
    for k in range(7):
        scatter(k).wait_send()
    for p in (0, 1):
        for ref, sem in (
            (own_z.at[p], sz_s), (own_m.at[p], sm_s), (own_z.at[p], zz_s), (own_m.at[p, pl.ds(1, OWNERS - 1)], rg_s)
        ):
            pltpu.make_async_copy(ref, ref, sem.at[p]).wait()


def reduce_tables(part):
    bf = jnp.bfloat16
    n = OWNERS
    return pl.pallas_call(
        reduce_kernel,
        out_shape=jax.ShapeDtypeStruct((ROWS, 128), bf),
        in_specs=[pl.BlockSpec(memory_space=pl.ANY)],
        out_specs=pl.BlockSpec(memory_space=pl.ANY),
        scratch_shapes=[
            pltpu.VMEM((2, n, PAIR, 128), bf), pltpu.VMEM((2, n, SUB, 128), bf),
            pltpu.VMEM((2, n, PAIR, 128), bf), pltpu.VMEM((2, n, SUB, 128), bf),
            pltpu.VMEM((2, n, PAIR, 128), bf), pltpu.VMEM((2, n, SUB, 128), bf),
            pltpu.VMEM((2, PAIR, 128), bf), pltpu.VMEM((7, CHUNK, 128), bf), pltpu.VMEM((CHUNK, 128), bf),
        ] + [dma(2, n)] * 2 + [dma(2), dma(2, n)] * 4 + [dma(7)] * 2 + [dma(ZS)] * 4 + [dma()],
        compiler_params=pltpu.CompilerParams(collective_id=3, has_side_effects=True, vmem_limit_bytes=56 * 1024 * 1024),
        cost_estimate=pl.CostEstimate(flops=0, bytes_accessed=50000000, transcendentals=0),
        name="reduce_tables",
    )(part)


learn_rate = 0.1


def body(
    dense_input,
    owner_route,
    local_row,
    labels,
    table_rows,
    adagrad_state,
    cross_down,
    cross_up,
    cross_bias,
    out_weight,
):
    samples = dense_input.shape[0]
    tables = local_row.shape[1]
    lookups = samples * tables
    ids = (owner_route.reshape(samples, tables) * ROWS + local_row).T.reshape(lookups)
    fetched = gather_tables(table_rows.astype(jnp.bfloat16))[ids]
    logits, partial_rows = cross_layer(
        ids, dense_input, fetched, labels[:, None], cross_down, cross_up, cross_bias[None, :], out_weight[None, :]
    )
    row_grad = reduce_tables(partial_rows).astype(jnp.float32)
    fresh_state = adagrad_state + jnp.mean(row_grad * row_grad, axis=1)
    new_rows = table_rows - learn_rate * row_grad / jnp.sqrt(fresh_state)[:, None]
    return (new_rows, logits.reshape(samples))


def solution(mesh):
    in_specs = (
        P(("owner", "hst"), None),
        P(("owner", "hst"), None, None),
        P(("owner", "hst"), None),
        P(("owner", "hst")),
        P("owner", None),
        P("owner"),
        P(),
        P(),
        P(),
        P(),
    )
    out_specs = (P("owner", None), P(("owner", "hst")))
    return jax.shard_map(body, mesh=mesh, in_specs=in_specs, out_specs=out_specs, check_vma=False)
```

```python
import heapq
import jax
import jax.numpy as jnp
from jax import lax
from jax.experimental import pallas as pl
from jax.experimental.pallas import tpu as pltpu
from jax.sharding import PartitionSpec as P

XS, YS, ZS, OWNERS = 4, 8, 12, 32
ROWS = 3072
HALF, PAIR, SUB = 1536, 512, 256
TABLE = OWNERS * ROWS
STEPS = ((1, 0), (-1, 0), (0, 1), (0, -1))


def trees():
    children = [[[] for _ in range(OWNERS)] for _ in range(2)]

    def grow(plan, parent, direction):
        i, j = parent[0] + STEPS[direction][0], parent[1] + STEPS[direction][1]
        children[plan][parent[0] % XS * YS + parent[1] % YS].append((i % XS * YS + j % YS, direction))
        return i, j

    def line(plan, start, direction, count):
        for _ in range(count):
            start = grow(plan, start, direction)
        return start

    def over_x(plan, start, up):
        line(plan, start, 0, up)
        line(plan, start, 1, 3 - up)

    over_x(0, (0, 0), 2)
    for i in range(XS):
        far = line(0, (i, 0), 2, 4 if i == 0 else 3)
        line(0, (i, 0), 3, 3)
        if i == 0:
            over_x(0, far, 1)
    line(1, (0, 0), 2, 3)
    line(1, (0, 0), 3, 4)
    for j in range(YS):
        over_x(1, (0, j), 2 - j % 2)
    return children


def depths(children, n):
    return 1 + max([depths(children, m) for m, _ in children[n]], default=0)


TIME, DELAY = 2.85, 4.0


def schedule(children):
    waiting, busy, events, steps = [[] for _ in STEPS], [False] * 4, [(0.0, 0, 0, 0), (0.0, 1, 1, 0)], []
    while events:
        now, _, plan, n = heapq.heappop(events)
        if plan < 0:
            busy[n] = False
        else:
            if n:
                steps.append((now, 0, len(steps), (plan, n)))
            for m, direction in children[plan][n]:
                heapq.heappush(waiting[direction], (-depths(children[plan], m), now, len(steps), m, plan, n))
        for direction in range(4):
            if waiting[direction] and not busy[direction]:
                _, ready, _, m, p, parent = heapq.heappop(waiting[direction])
                busy[direction] = True
                steps.append((max(ready, now - TIME), 1, len(steps), (p, parent, m, direction)))
                heapq.heappush(events, (now + TIME, 1000 + direction, -1, direction))
                heapq.heappush(events, (now + TIME + DELAY, 2000 + len(steps), p, m))
    return [step[3] for step in sorted(steps)]


TREES = trees()
SCHEDULE = schedule(TREES)
ORDER = [step for step in SCHEDULE if len(step) == 2]


def place():
    o = lax.axis_index("owner")
    h = lax.axis_index("hst")
    x, y, z, core = o // YS, o % YS, h // 2, h % 2
    near = [(((x + i + XS) % XS) * YS + (y + j + YS) % YS, h) for i, j in STEPS]
    owners = [((x + XS - n // YS) % XS) * YS + (y + YS - n % YS) % YS for n in range(OWNERS)]
    return o, h, z, core, near, owners


def greet(devices):
    barrier = pltpu.get_barrier_semaphore()
    for d in devices:
        pl.semaphore_signal(barrier, inc=1, device_id=d, device_id_type=pl.DeviceIdType.MESH)
    pl.semaphore_wait(barrier, len(devices))


def send(src, dst, ssem, rsem, device):
    return pltpu.make_async_remote_copy(
        src_ref=src, dst_ref=dst, send_sem=ssem, recv_sem=rsem,
        device_id=device, device_id_type=pl.DeviceIdType.MESH)


Z_LAG = 14


def gather_kernel(tab, out, own_sem, ring_s, ring_r, sib_s, sib_r, z_s, z_r, zs_s, zs_r):
    o, h, z, core, near, owners = place()
    color = z % 3
    sib = (o, h + 1 - 2 * core)
    zdev = [(o, ((z + 1) % ZS) * 2 + core), (o, ((z + ZS - 1) % ZS) * 2 + core)]
    greet([sib] + zdev + near)
    base = core * HALF
    pair_row = [base + ((color + 1) % 3) * PAIR, base + ((color + 2) % 3) * PAIR]
    miss_row = [base + color * PAIR, base + color * PAIR + SUB]

    own = pltpu.make_async_copy(tab, out.at[pl.ds(pl.multiple_of(o * ROWS, ROWS), ROWS)], own_sem)
    own.start()

    def rows(n, row, count):
        return out.at[pl.ds(pl.multiple_of(owners[n] * ROWS + row, SUB), count)]

    def ring(p, n, m, direction):
        ref = rows(n, pair_row[p], PAIR)
        src = ref if n else tab.at[pl.ds(pl.multiple_of(pair_row[p], SUB), PAIR)]
        return send(src, ref, ring_s.at[p], ring_r.at[p, m], near[direction])

    def sibling(p, n):
        ref = rows(n, pair_row[p], PAIR)
        return send(ref, ref, sib_s.at[p], sib_r.at[p], sib)

    def zed(p, n):
        ref = rows(n, pair_row[p] + p * SUB, SUB)
        return send(ref, ref, z_s.at[p], z_r.at[p, n], zdev[p])

    def zsib(p, n):
        ref = rows(n, miss_row[p], SUB)
        return send(ref, ref, zs_s.at[p], zs_r.at[p], sib)

    def await_(ref, sem):
        pltpu.make_async_copy(ref, ref, sem).wait()

    def from_z(p, n):
        await_(rows(n, miss_row[p], SUB), z_r.at[p, n])
        zsib(p, n).start()

    came = []
    for step in SCHEDULE:
        if len(step) == 4:
            ring(*step).start()
            continue
        p, n = step
        await_(rows(n, pair_row[p], PAIR), ring_r.at[p, n])
        came.append(step)
        zed(p, n).start()
        sibling(p, n).start()
        if len(came) > Z_LAG:
            from_z(*came[-1 - Z_LAG])
    for step in came[-Z_LAG:]:
        from_z(*step)
    whole, half = out.at[pl.ds(0, 31 * PAIR)], out.at[pl.ds(0, 31 * SUB)]
    for p in (0, 1):
        await_(whole, sib_r.at[p])
        await_(half, zs_r.at[p])
        for sem in (ring_s, sib_s):
            await_(whole, sem.at[p])
        for sem in (z_s, zs_s):
            await_(half, sem.at[p])
    own.wait()


def dma(*shape):
    return pltpu.SemaphoreType.DMA(shape)


def gather_tables(tab):
    return pl.pallas_call(
        gather_kernel,
        out_shape=jax.ShapeDtypeStruct((TABLE, 128), jnp.bfloat16),
        in_specs=[pl.BlockSpec(memory_space=pl.ANY)],
        out_specs=pl.BlockSpec(memory_space=pl.ANY),
        scratch_shapes=[dma()] + [dma(2), dma(2, OWNERS), dma(2), dma(2), dma(2), dma(2, OWNERS), dma(2), dma(2)],
        compiler_params=pltpu.CompilerParams(collective_id=2, has_side_effects=True),
        cost_estimate=pl.CostEstimate(flops=0, bytes_accessed=50000000, transcendentals=0),
        name="gather_tables",
    )(tab)


LOOKUPS = 6656


def scatter_kernel(ids, g, out, acc, gf, stage, sem):
    def clear(i, _):
        acc[pl.ds(pl.multiple_of(i * 1024, 1024), 1024), :] = jnp.zeros((1024, 128), jnp.float32)
        return 0
    lax.fori_loop(0, TABLE // 1024, clear, 0)

    def widen(i, _):
        r = pl.ds(pl.multiple_of(i * 128, 128), 128)
        gf[r, :] = g[r, :].astype(jnp.float32)
        return 0
    lax.fori_loop(0, LOOKUPS // 128, widen, 0)

    def add(i, _):
        for k in range(16):
            j = i * 16 + k
            row = ids[j]
            acc[pl.ds(row, 1), :] = acc[pl.ds(row, 1), :] + gf[pl.ds(j, 1), :]
        return 0
    lax.fori_loop(0, LOOKUPS // 16, add, 0)

    def copy(i):
        slot = i % 2
        return pltpu.make_async_copy(stage.at[slot], out.at[pl.ds(pl.multiple_of(i * ROWS, ROWS), ROWS)], sem.at[slot])

    def write(i, _):
        @pl.when(i >= 2)
        def _():
            copy(i - 2).wait()

        def narrow(k, _):
            r = pl.multiple_of(k * 512, 512)
            stage[i % 2, pl.ds(r, 512), :] = acc[pl.ds(pl.multiple_of(i * ROWS + r, 512), 512), :].astype(jnp.bfloat16)
            return 0
        lax.fori_loop(0, ROWS // 512, narrow, 0)
        copy(i).start()
        return 0
    lax.fori_loop(0, OWNERS, write, 0)
    copy(OWNERS - 2).wait()
    copy(OWNERS - 1).wait()


def scatter_rows(ids, g):
    return pl.pallas_call(
        scatter_kernel,
        out_shape=jax.ShapeDtypeStruct((TABLE, 128), jnp.bfloat16),
        in_specs=[pl.BlockSpec(memory_space=pltpu.SMEM), pl.BlockSpec(memory_space=pltpu.VMEM)],
        out_specs=pl.BlockSpec(memory_space=pl.ANY),
        scratch_shapes=[
            pltpu.VMEM((TABLE, 128), jnp.float32), pltpu.VMEM((LOOKUPS, 128), jnp.float32),
            pltpu.VMEM((2, ROWS, 128), jnp.bfloat16), pltpu.SemaphoreType.DMA((2,))],
        compiler_params=pltpu.CompilerParams(vmem_limit_bytes=60 * 1024 * 1024),
        name="scatter_rows",
    )(ids, g)


CHUNK = 128
LOAD_AHEAD, Z_AHEAD = 20, 14
BACK = [e for e in reversed(ORDER)] + [(0, 0), (1, 0)]


def reduce_kernel(part, out, own_m, own_z, sib_m, sib_z, ring_b, z_b, fin, zr, tot,
                  lm, lz, sm_s, sm_r, sz_s, sz_r, rg_s, rg_r, zz_s, zz_r, c_s, c_r, b_s, b_r, f_s, f_r, t_s):
    o, h, z, core, near, owners = place()
    color = z % 3
    sib = (o, h + 1 - 2 * core)
    zs = [(o, ((z + k) % ZS) * 2 + core) for k in range(ZS)]
    greet([sib] + zs[1:] + near)
    zdev = [zs[ZS - 1], zs[1]]
    pair = [((color + 1) % 3) * PAIR, ((color + 2) % 3) * PAIR]
    miss = [color * PAIR, color * PAIR + SUB]

    def src(n, side, row, count):
        return part.at[pl.ds(pl.multiple_of(owners[n] * ROWS + side * HALF + row, SUB), count)]

    def load_z(p, n):
        return pltpu.make_async_copy(src(n, core, miss[p], SUB), own_z.at[p, n], lz.at[p, n])

    def load_m(p, n):
        return pltpu.make_async_copy(src(n, core, pair[p], PAIR), own_m.at[p, n], lm.at[p, n])

    def give_z(p, n):
        return send(src(n, 1 - core, miss[p], SUB), sib_z.at[p, n], sz_s.at[p], sz_r.at[p, n], sib)

    def give_m(p, n):
        return send(src(n, 1 - core, pair[p], PAIR), sib_m.at[p, n], sm_s.at[p], sm_r.at[p, n], sib)

    def zcopy(p, n):
        return send(own_z.at[p, n], z_b.at[p, n], zz_s.at[p], zz_r.at[p, n], zdev[p])

    def rcopy(p, n, direction):
        return send(own_m.at[p, n], ring_b.at[p, n], rg_s.at[p], rg_r.at[p, n], near[direction ^ 1])

    reached = [{m: d for l in TREES[p] for m, d in l} for p in (0, 1)]

    def fetch(p, n):
        for make in (give_z, load_z, give_m, load_m):
            make(p, n).start()

    def zpart(p, n):
        load_z(p, n).wait()
        give_z(p, n).wait_recv()

        def add(i, _):
            r = pl.ds(pl.multiple_of(i * 128, 128), 128)
            own_z[p, n, r, :] = (own_z[p, n, r, :].astype(jnp.float32) + sib_z[p, n, r, :].astype(jnp.float32)).astype(jnp.bfloat16)
            return 0
        lax.fori_loop(0, SUB // 128, add, 0)
        zcopy(p, n).start()

    def total(p, n):
        load_m(p, n).wait()
        give_m(p, n).wait_recv()
        zcopy(p, n).wait_recv()
        for m, direction in TREES[p][n]:
            rcopy(p, m, direction).wait_recv()

        def add(i, _, with_z, first):
            r = pl.ds(pl.multiple_of(first + i * 128, 128), 128)
            t = own_m[p, n, r, :].astype(jnp.float32) + sib_m[p, n, r, :].astype(jnp.float32)
            if with_z:
                t = t + z_b[p, n, pl.ds(pl.multiple_of(i * 128, 128), 128), :].astype(jnp.float32)
            for m, _direction in TREES[p][n]:
                t = t + ring_b[p, m, r, :].astype(jnp.float32)
            t = t.astype(jnp.bfloat16)
            if n == 0:
                fin[p, r, :] = t
            else:
                own_m[p, n, r, :] = t
            return 0
        lax.fori_loop(0, SUB // 128, lambda i, x: add(i, x, p == 0, 0), 0)
        lax.fori_loop(0, SUB // 128, lambda i, x: add(i, x, p == 1, SUB), 0)
        if n:
            rcopy(p, n, reached[p][n]).start()

    for k in range(-LOAD_AHEAD, len(BACK)):
        if k == -LOAD_AHEAD:
            for e in BACK[:LOAD_AHEAD]:
                fetch(*e)
        if 0 <= k and k + LOAD_AHEAD < len(BACK):
            fetch(*BACK[k + LOAD_AHEAD])
        if -Z_AHEAD <= k and k + Z_AHEAD < len(BACK):
            zpart(*BACK[k + Z_AHEAD])
        if k >= 0:
            total(*BACK[k])

    hops = [3, 6, 9, 1, 4, 7, 10]

    def scatter(k):
        hop = hops[k]
        to = (z + hop) % ZS
        ref = fin.at[0 if k < 3 else 1, pl.ds(pl.multiple_of((to // 3) * CHUNK, CHUNK), CHUNK)]
        return send(ref, zr.at[k], c_s.at[k], c_r.at[k], zs[hop])
    for k in (1, 4, 5, 0, 2, 6, 3):
        scatter(k).start()
    mine = pl.ds(pl.multiple_of((z // 3) * CHUNK, CHUNK), CHUNK)
    for k in range(7):
        scatter(k).wait_recv()
    t = fin[0, mine, :].astype(jnp.float32)
    for k in range(7):
        t = t + zr[k].astype(jnp.float32)
    tot[...] = t.astype(jnp.bfloat16)

    def chunk_rows(layer):
        return out.at[pl.ds(pl.multiple_of(core * HALF + ((layer % 3 + 1) % 3) * PAIR + (layer // 3) * CHUNK, CHUNK), CHUNK)]

    def spread(k):
        return send(tot, chunk_rows(z), b_s.at[k], b_r.at[k], zs[k])

    def arrived(k):
        ref = chunk_rows((z + ZS - k) % ZS)
        return send(ref, ref, f_s.at[k], f_r.at[k], sib)

    far = [6, 5, 7, 4, 8, 3, 9, 2, 10, 1, 11]
    near_first = far[::-1]
    for k in far:
        spread(k).start()
    first = send(tot, chunk_rows(z), f_s.at[0], f_r.at[0], sib)
    first.start()
    keep = pltpu.make_async_copy(tot, chunk_rows(z), t_s)
    keep.start()
    for k in near_first:
        ref = chunk_rows((z + ZS - k) % ZS)
        pltpu.make_async_copy(ref, ref, b_r.at[k]).wait()
        arrived(k).start()
    keep.wait()
    first.wait()
    for k in far:
        spread(k).wait_send()
        arrived(k).wait()
    for k in range(7):
        scatter(k).wait_send()
    for p in (0, 1):
        for ref, sem in (
            (own_z.at[p], sz_s), (own_m.at[p], sm_s), (own_z.at[p], zz_s), (own_m.at[p, pl.ds(1, OWNERS - 1)], rg_s)
        ):
            pltpu.make_async_copy(ref, ref, sem.at[p]).wait()


def reduce_tables(part):
    bf = jnp.bfloat16
    n = OWNERS
    return pl.pallas_call(
        reduce_kernel,
        out_shape=jax.ShapeDtypeStruct((ROWS, 128), bf),
        in_specs=[pl.BlockSpec(memory_space=pl.ANY)],
        out_specs=pl.BlockSpec(memory_space=pl.ANY),
        scratch_shapes=[
            pltpu.VMEM((2, n, PAIR, 128), bf), pltpu.VMEM((2, n, SUB, 128), bf),
            pltpu.VMEM((2, n, PAIR, 128), bf), pltpu.VMEM((2, n, SUB, 128), bf),
            pltpu.VMEM((2, n, PAIR, 128), bf), pltpu.VMEM((2, n, SUB, 128), bf),
            pltpu.VMEM((2, PAIR, 128), bf), pltpu.VMEM((7, CHUNK, 128), bf), pltpu.VMEM((CHUNK, 128), bf),
        ] + [dma(2, n)] * 2 + [dma(2), dma(2, n)] * 4 + [dma(7)] * 2 + [dma(ZS)] * 4 + [dma()],
        compiler_params=pltpu.CompilerParams(collective_id=3, has_side_effects=True, vmem_limit_bytes=56 * 1024 * 1024),
        cost_estimate=pl.CostEstimate(flops=0, bytes_accessed=50000000, transcendentals=0),
        name="reduce_tables",
    )(part)


NT = (((1,), (1,)), ((), ()))


def cross_kernel(dense, fetched, labels, down_hbm, up_hbm, bias, weight, logits, grads, joined, mixed, down, up, sem):
    samples = dense.shape[0]
    take_down = pltpu.make_async_copy(down_hbm, down, sem.at[0])
    take_up = pltpu.make_async_copy(up_hbm, up, sem.at[1])
    take_down.start()
    take_up.start()
    joined[:, 0:128] = dense[...]
    for t in range(26):
        joined[:, 128 * (t + 1):128 * (t + 2)] = fetched[samples * t:samples * (t + 1), :]

    def columns(i, width):
        return pl.ds(pl.multiple_of(i * width, 128), width)

    take_down.wait()

    def first(i, acc):
        c = columns(i, 1152)
        return acc + jnp.dot(joined[:, c], down[c, :], preferred_element_type=jnp.float32)
    lowrank = lax.fori_loop(0, 3, first, jnp.zeros((samples, 512), jnp.float32)).astype(jnp.bfloat16)

    take_up.wait()

    def second(i, acc):
        c = columns(i, 384)
        m = 1.0 + (jnp.dot(lowrank, up[:, c], preferred_element_type=jnp.float32) + bias[:, c])
        mixed[:, c] = m
        v = joined[:, c].astype(jnp.float32) * m * weight[:, c]
        return acc + (v[:, 0:128] + v[:, 128:256] + v[:, 256:384])
    acc = lax.fori_loop(0, 9, second, jnp.zeros((samples, 128), jnp.float32))
    logit = jnp.sum(acc, axis=1, keepdims=True)
    logits[...] = logit
    slope = jax.nn.sigmoid(logit) - labels[...].astype(jnp.float32)

    def third(i, acc):
        c = columns(i, 1152)
        s = (slope * weight[:, c] * joined[:, c].astype(jnp.float32)).astype(jnp.bfloat16)
        return acc + lax.dot_general(s, up[:, c], NT, preferred_element_type=jnp.float32)
    back = lax.fori_loop(0, 3, third, jnp.zeros((samples, 512), jnp.float32)).astype(jnp.bfloat16)

    def fourth(i, _):
        c = pl.ds(pl.multiple_of(128 + i * 256, 128), 256)
        e = slope * weight[:, c] * mixed[:, c] + lax.dot_general(
            back, down[c, :], NT, preferred_element_type=jnp.float32)
        e = e.astype(jnp.bfloat16)
        r = pl.multiple_of(i * 2 * samples, 512)
        grads[pl.ds(r, samples), :] = e[:, 0:128]
        grads[pl.ds(r + samples, samples), :] = e[:, 128:256]
        return 0
    lax.fori_loop(0, 13, fourth, 0)


def cross_layer(dense, fetched, labels, down, up, bias, weight):
    samples = dense.shape[0]
    vmem = pl.BlockSpec(memory_space=pltpu.VMEM)
    return pl.pallas_call(
        cross_kernel,
        out_shape=(
            jax.ShapeDtypeStruct((samples, 1), jnp.float32),
            jax.ShapeDtypeStruct(fetched.shape, jnp.bfloat16)),
        in_specs=[vmem] * 3 + [pl.BlockSpec(memory_space=pl.ANY)] * 2 + [vmem] * 2,
        out_specs=[vmem] * 2,
        scratch_shapes=[pltpu.VMEM((samples, 3456), jnp.bfloat16), pltpu.VMEM((samples, 3456), jnp.float32),
                        pltpu.VMEM(down.shape, jnp.bfloat16), pltpu.VMEM(up.shape, jnp.bfloat16), dma(2)],
        compiler_params=pltpu.CompilerParams(vmem_limit_bytes=60 * 1024 * 1024),
        name="cross_layer",
    )(dense, fetched, labels, down, up, bias, weight)


learn_rate = 0.1


def body(
    dense_input,
    owner_route,
    local_row,
    labels,
    table_rows,
    adagrad_state,
    cross_down,
    cross_up,
    cross_bias,
    out_weight,
):
    samples = dense_input.shape[0]
    tables = local_row.shape[1]
    lookups = samples * tables
    ids = (owner_route.reshape(samples, tables) * ROWS + local_row).T.reshape(lookups)
    fetched = gather_tables(table_rows.astype(jnp.bfloat16))[ids]
    logits, emb_grad = cross_layer(
        dense_input, fetched, labels[:, None], cross_down, cross_up, cross_bias[None, :], out_weight[None, :]
    )
    row_grad = reduce_tables(scatter_rows(ids, emb_grad)).astype(jnp.float32)
    fresh_state = adagrad_state + jnp.mean(row_grad * row_grad, axis=1)
    new_rows = table_rows - learn_rate * row_grad / jnp.sqrt(fresh_state)[:, None]
    return (new_rows, logits.reshape(samples))


def solution(mesh):
    in_specs = (
        P(("owner", "hst"), None),
        P(("owner", "hst"), None, None),
        P(("owner", "hst"), None),
        P(("owner", "hst")),
        P("owner", None),
        P("owner"),
        P(),
        P(),
        P(),
        P(),
    )
    out_specs = (P("owner", None), P(("owner", "hst")))
    return jax.shard_map(body, mesh=mesh, in_specs=in_specs, out_specs=out_specs, check_vma=False)
```
